256 devices in a mesh: ctx: 64 (over z, x, core), head: 4 (over y).
Axes of the slice: x: 4, y: 4, z: 8, core: 2. Of those that a mesh axis runs over, the one named last changes fastest.
Arguments:
- queries: bfloat16 [65536, 2048], P('ctx', 'head'), may hold values from -6 to 6
- keys: bfloat16 [65536, 2048], P('ctx', 'head'), may hold values from -6 to 6
- values: bfloat16 [65536, 4096], P('ctx', 'head'), may hold values from -6 to 6
- log_gate: bfloat16 [65536, 2048], P('ctx', 'head'), may hold values from -1.7 to 0, as said below
- out_gate: bfloat16 [65536, 4096], P('ctx', 'head'), may hold values from -6 to 6
- segment_ids: int32 [512], replicated, may hold values from 0 to 3, never falling along the last dimension, each value on 1 to 256 neighbouring positions
- final_projector: bfloat16 [4096, 4096], P('head'), may hold values from -0.09375 to 0.09375
Outputs:
- projected: bfloat16 [65536, 4096], P('ctx', 'head')
The draws below stay inside these ranges and needn't reach their ends.
Inputs may be any that keep to these rules, and one draw needn't show every extreme that they name: `segment_ids`: segment numbers never fall; a segment spans at most 256 blocks. `log_gate`: logarithm of a decay factor.
All inputs are finite; a program needn't handle non-finite values.
Results may differ from the reference program's by a relative error of at most 0.013.
Values may be sent and summed in bfloat16 or wider, within the bound.
A program may use at most 192 MiB of HBM per device.

```python
import math
import jax
import jax.numpy as jnp
import numpy as np
from jax import lax

D = 4096
HEAD_DEV = 4
DK = 128
DV = 256
CH = 128
HEADS = 16
TOKENS = 65536
STRETCHES = 512


def draw_log_gate(key, part):
    subkeys = jax.random.split(key, 5)
    width = HEADS * DK
    slow_count = 5
    slow_head = jax.random.randint(subkeys[0], (HEADS,), 0, 10) < slow_count
    slow_channel = jnp.repeat(slow_head, DK)
    picked = jax.random.uniform(subkeys[1], (width,), jnp.float32)
    slow_rate = jnp.exp(jnp.log(0.05) + picked * jnp.log(12.0)) / TOKENS
    fast_rate = jnp.exp(jnp.log(0.02) + picked * jnp.log(50.0 / 30.0))
    default_forget_factor = jnp.where(slow_channel, slow_rate, fast_rate)
    crude_guess = jnp.exp(jax.random.uniform(subkeys[2], (TOKENS, width), jnp.float32, jnp.log(0.5), jnp.log(2.0)))
    boundary_offsets = jax.random.randint(subkeys[3], (3,), 0, TOKENS)
    utterance_level_numbers = jax.random.uniform(subkeys[4], (3,), jnp.float32, 0.2, 0.4)
    sequence_slot = jnp.arange(TOKENS)
    utterance_span_size = jnp.sum(jnp.where(sequence_slot[:, None] == boundary_offsets[None, :], jnp.log(1.0 - utterance_level_numbers)[None, :], 0.0), axis=1)
    return (-default_forget_factor[None, :] * crude_guess + utterance_span_size[:, None]).astype(jnp.bfloat16)


def shard_levels(rng, extent, pieces, smallest, high):
    gain = 1.0
    for axis_at, shards_of in pieces:
        heights = jax.random.uniform(jax.random.fold_in(jax.random.fold_in(rng, 6), axis_at), (shards_of,), jnp.float32, smallest / len(pieces), high / len(pieces))
        gain = gain * jnp.repeat(jnp.exp(heights), extent[axis_at] // shards_of).reshape((-1,) + (1,) * (len(extent) - 1 - axis_at))
    return gain


def split_up(number_of, total, bound, lean):
    portions = [(1 << 20) // math.isqrt(standing ** lean) + 1 for standing in range(2, number_of + 1)]
    rest, holding = total - bound - (number_of - 1), [1] * (number_of - 1)
    while rest > 0:
        candidates = [i for i in range(number_of - 1) if holding[i] < bound]
        pool, remaining = sum([portions[i] for i in candidates]), rest
        for i in candidates:
            addition = min(bound - holding[i], max(1, remaining * portions[i] // pool), rest)
            holding[i] = holding[i] + addition
            rest = rest - addition
    return np.array([bound] + holding)


def ragged_sizes(rng, amount, total, bound, lean):
    if amount == 2:
        one = jax.random.randint(rng, (), max(1, total - bound), min(bound, total - 1) + 1)
        return jnp.stack([one, total - one])
    sizes = jnp.asarray(split_up(amount, total, bound, lean), jnp.int32)
    pairs = (amount - 1) // 2
    donor, receiver = sizes[1:1 + 2 * pairs:2], sizes[2:2 + 2 * pairs:2]
    slack = jnp.minimum(donor - 1, bound - receiver)
    passed = jax.random.randint(jax.random.fold_in(rng, 1), (pairs,), 0, 1 << 20) % (slack + 1)
    sizes = sizes.at[1:1 + 2 * pairs:2].set(donor - passed).at[2:2 + 2 * pairs:2].set(receiver + passed)
    return sizes[jax.random.permutation(jax.random.fold_in(rng, 2), amount)]


def centred(key, extent, spread, limit, cuts=(), dtype=jnp.bfloat16):
    drawn = spread * jax.random.normal(key, extent, jnp.float32)
    if cuts:
        drawn = drawn * shard_levels(key, extent, cuts, -0.22, 0.18)
    return jnp.clip(drawn, -limit, limit).astype(dtype)


def setup_inputs(seed: int = 0) -> dict:
    arg_keys = jax.random.split(jax.random.key(seed), 8)
    return {
        "queries": centred(arg_keys[0], (TOKENS, HEADS * DK), 1.0, 6.0, ((0, 64), (1, 4))),
        "keys": centred(arg_keys[1], (TOKENS, HEADS * DK), 1.0, 6.0, ((0, 64), (1, 4))),
        "values": centred(arg_keys[2], (TOKENS, HEADS * DV), 1.0, 6.0, ((0, 64), (1, 4))),
        "log_gate": draw_log_gate(jax.random.fold_in(arg_keys[7], 71), 0),
        "out_gate": centred(arg_keys[4], (TOKENS, HEADS * DV), 1.0, 6.0, ((0, 64), (1, 4))),
        "segment_ids": jnp.searchsorted(jnp.cumsum(ragged_sizes(arg_keys[5], 4, STRETCHES, STRETCHES // 2, 0)), jnp.arange(STRETCHES), side="right").astype(jnp.int32),
        "final_projector": centred(arg_keys[6], (HEADS * DV, D), (HEADS * DV) ** -0.5, 0.09375, ((0, 4),)),
    }


def reference(queries, keys, values, log_gate, out_gate, segment_ids, final_projector):
    blocks = TOKENS // CH
    query_f = queries.astype(jnp.float32).reshape(blocks, CH, HEADS, DK)
    key_f = keys.astype(jnp.float32).reshape(blocks, CH, HEADS, DK)
    value_b = values.reshape(blocks, CH, HEADS, DV)
    rate_rows = log_gate.astype(jnp.float32).reshape(blocks, CH, HEADS, DK)
    earlier_ids = jnp.concatenate([segment_ids[:1] - 1, segment_ids[:-1]])
    keep_flags = (segment_ids == earlier_ids).astype(jnp.float32)
    row_ids = lax.broadcasted_iota(jnp.int32, (CH, CH), 0)
    col_ids = lax.broadcasted_iota(jnp.int32, (CH, CH), 1)
    causal = col_ids <= row_ids

    def block_step(state_now, single_entry):
        query_b, key_b, value_one, rate_b, keep_one = single_entry
        running = jnp.cumsum(rate_b, axis=0)
        final_sum = running[-1]
        state_now = keep_one * state_now
        decayed_q = query_b * jnp.exp(running) * DK ** (-0.5)
        decayed_k = key_b * jnp.exp(-running)
        scores = jnp.einsum('ihc,jhc->hij', decayed_q, decayed_k, precision=lax.Precision.HIGHEST)
        probs_bf = jnp.where(causal[None], scores, 0.0).astype(jnp.bfloat16)
        within_block_output = jnp.einsum('hij,jhd->ihd', probs_bf.astype(jnp.float32), value_one.astype(jnp.float32))
        carried = jnp.einsum('ihc,hcd->ihd', decayed_q, state_now, precision=lax.Precision.HIGHEST)
        kept_k = (key_b * jnp.exp(final_sum[None] - running)).astype(jnp.bfloat16)
        local_terms = jnp.einsum('jhc,jhd->hcd', kept_k.astype(jnp.float32), value_one.astype(jnp.float32))
        new_state = jnp.exp(final_sum)[:, :, None] * state_now + local_terms
        return (new_state, carried + within_block_output)
    start_state = jnp.zeros((HEADS, DK, DV), jnp.float32)
    _, mixed_out = lax.scan(block_step, start_state, (query_f, key_f, value_b, rate_rows, keep_flags))
    mixed_out = mixed_out.reshape(TOKENS, HEADS, DV)
    scaled = mixed_out * lax.rsqrt(lax.optimization_barrier(jnp.mean(mixed_out * mixed_out, axis=-1, keepdims=True)) + 1e-05)
    gate_vals = out_gate.astype(jnp.float32).reshape(TOKENS, HEADS, DV)
    latent_width = (scaled * jax.nn.silu(gate_vals)).astype(jnp.bfloat16)
    groups = HEADS // HEAD_DEV
    flat = latent_width.reshape(TOKENS, groups, HEAD_DEV * DV)
    weight_groups = final_projector.reshape(groups, HEAD_DEV * DV, D)
    total = jnp.zeros((TOKENS, D), jnp.float32)
    for group in range(groups):
        part_out = jnp.dot(flat[:, group], weight_groups[group], preferred_element_type=jnp.float32).astype(jnp.bfloat16)
        part_out = lax.optimization_barrier(part_out)
        total = total + part_out.astype(jnp.float32)
    return total.astype(jnp.bfloat16)
```

```python
import jax
import jax.numpy as jnp
from jax import lax
from jax.experimental import pallas as pl
from jax.experimental.pallas import tpu as pltpu
from jax.sharding import PartitionSpec as P

DK = 128
DV = 256
CH = 128
F32 = jnp.float32
BF16 = jnp.bfloat16
MESH = pl.DeviceIdType.MESH

NX = 4
NZ = 8
REACH = 4


def dot(a, b, dims):
    return lax.dot_general(a, b, (dims, ((), ())), preferred_element_type=F32)


def local_kernel(keep, q, k, v, g, mixed, reach_q, state_out, decay_out, state, weight):
    b = pl.program_id(0)
    heads = q.shape[1] // DK

    @pl.when(b == 0)
    def _():
        state[...] = jnp.zeros_like(state)
        weight[...] = jnp.ones_like(weight)

    keep_b = keep[b]
    rows = lax.broadcasted_iota(jnp.int32, (CH, CH), 0)
    cols = lax.broadcasted_iota(jnp.int32, (CH, CH), 1)
    causal = cols <= rows
    cum = dot(causal.astype(F32).astype(BF16), g[...], ((1,), (0,)))
    last = cum[CH - 1 : CH, :]
    qf = q[...].astype(F32)
    kf = k[...].astype(F32)
    dq = qf * jnp.exp(cum) * DK ** (-0.5)
    dk = (kf * jnp.exp(-cum)).astype(BF16)
    kept = (kf * jnp.exp(last - cum)).astype(BF16)
    decay = jnp.exp(last)
    w = weight[...] * keep_b
    reach_q[...] = (dq * w).astype(BF16)
    weight[...] = w * decay
    dq = dq.astype(BF16)
    for h in range(heads):
        kc = slice(h * DK, (h + 1) * DK)
        vc = slice(h * DV, (h + 1) * DV)
        scores = dot(dq[:, kc], dk[:, kc], ((1,), (1,)))
        probs = jnp.where(causal, scores, 0.0).astype(BF16)
        start = state[:, kc] * keep_b
        out = dot(probs, v[:, vc], ((1,), (0,)))
        out += dot(dq[:, kc], start.astype(BF16), ((1,), (1,)))
        mixed[:, vc] = out.astype(BF16)
        local = dot(v[:, vc], kept[:, kc], ((0,), (0,)))
        state[:, kc] = start * decay[:, kc] + local

    @pl.when(b == pl.num_programs(0) - 1)
    def _():
        state_out[...] = state[...].astype(BF16)
        decay_out[...] = weight[...]


def exchange_kernel(
    state, decay, mixed_h, reach_h, gate_h, proj_h, out_h,
    mixed, reach, gate, wo, wp, hid, hid_peer, send, recv, res, own,
    p1, a1, xs, acc, t_out, a_out, t_in, a_in, plane, p3, e_in,
    s_p1, r_p1, s_a1, r_a1, s_p2, r_p2, s_a2, r_a2, s_p3, r_p3,
    s_w1, r_w1, s_wx, r_wx, s_wf, r_wf, s_ws, r_ws,
    s_hid, r_hid, s_rs, r_rs, s_load, s_out,
):
    ctx = lax.axis_index("ctx")
    y = lax.axis_index("head")
    z = ctx // (2 * NX)
    me = ctx % (2 * NX)
    x = me // 2
    core = me % 2
    base = z * (2 * NX)
    pair = y + 1 - 2 * (y % 2)
    over = 3 - y
    xr = (x + 1) % NX
    xl = (x + NX - 1) % NX
    xo = (x + 2) % NX
    tokens = hid.shape[0]
    chunks = tokens // CH
    width = wo.shape[2]
    depth = wo.shape[1]
    slab = depth // (2 * NX)
    part = p1.shape[1]

    def rdma(src, dst, ssem, rsem, c, h):
        return pltpu.make_async_remote_copy(
            src_ref=src, dst_ref=dst, send_sem=ssem, recv_sem=rsem,
            device_id={"ctx": c, "head": h}, device_id_type=MESH,
        )

    def arrived(dst, ssem, rsem):
        rdma(dst, dst, ssem, rsem, ctx, pair).wait_recv()

    def left(src, ssem, rsem):
        rdma(src, src, ssem, rsem, ctx, pair).wait_send()

    mine_cols = pl.ds(pl.multiple_of(y * width, width), width)
    over_cols = pl.ds(pl.multiple_of(over * width, width), width)
    loads = [
        pltpu.make_async_copy(mixed_h, mixed, s_load.at[0]),
        pltpu.make_async_copy(reach_h, reach, s_load.at[1]),
        pltpu.make_async_copy(gate_h, gate, s_load.at[2]),
        pltpu.make_async_copy(proj_h.at[:, over_cols], wo.at[1], s_load.at[3]),
        pltpu.make_async_copy(proj_h.at[:, mine_cols], wo.at[0], s_load.at[4]),
    ]
    for load in loads:
        load.start()

    barrier = pltpu.get_barrier_semaphore()

    def greet(c, h):
        pl.semaphore_signal(barrier, inc=1, device_id={"ctx": c, "head": h}, device_id_type=MESH)

    greet(ctx, pair)
    greet(ctx, over)
    for step in range(1, 2 * NX):
        greet(base + (me + step) % (2 * NX), y)
    for far in range(1, REACH + 1):

        @pl.when(z + far < NZ)
        def _():
            greet(ctx + far * 2 * NX, y)

        @pl.when(z - far >= 0)
        def _():
            greet(ctx - far * 2 * NX, y)

    ahead = jnp.minimum(NZ - 1 - z, REACH)
    behind = jnp.minimum(z, REACH)
    pl.semaphore_wait(barrier, 2 * NX + 1 + ahead + behind)

    def rows_of(i):
        return pl.ds(pl.multiple_of(i * part, part), part)

    for step in range(1, 2 * NX):
        i = (me + step) % (2 * NX)
        rdma(decay, a1.at[me], s_a1.at[i], r_a1.at[me], base + i, y).start()
        rdma(state.at[rows_of(i), :], p1.at[me], s_p1.at[i], r_p1.at[me], base + i, y).start()
    p1[me] = state[rows_of(me), :]
    a1[me] = decay[...]

    def slab_of(xx, cc):
        return pl.ds(pl.multiple_of((xx * 2 + cc) * slab, slab), slab)

    def half_of(xx, cc, half):
        return pl.ds(pl.multiple_of((xx * 2 + cc) * slab + half * (slab // 2), slab // 2), slab // 2)

    pair_cols = (
        pl.ds(pl.multiple_of(pair * width, width), width),
        pl.ds(pl.multiple_of((3 - pair) * width, width), width),
    )
    here = slab_of(x, core)
    at_r = base + xr * 2 + core
    at_l = base + xl * 2 + core
    sib = base + x * 2 + 1 - core

    def w1(j):
        return rdma(proj_h.at[here, pair_cols[j]], wp.at[j, here], s_w1.at[j], r_w1.at[j], ctx, pair)

    def along(j, rows, s, r, item, to):
        return rdma(wp.at[j, rows], wp.at[j, rows], s.at[j, item], r.at[j, item], to, y)

    def wait_in(j, rows, s, r, item):
        arrived(wp.at[j, rows], s.at[j, item], r.at[j, item])

    def relays(cc):
        return (
            slab_of(x, cc), slab_of(xl, cc), slab_of(xr, cc), half_of(xo, cc, 0), half_of(xo, cc, 1),
        )

    def stage_a(j):
        arrived(wp.at[j, here], s_w1.at[j], r_w1.at[j])
        along(j, here, s_wx, r_wx, 0, at_r).start()
        along(j, here, s_wx, r_wx, 1, at_l).start()
        along(j, here, s_ws, r_ws, 0, sib).start()

    def stage_b(j):
        wait_in(j, slab_of(xl, core), s_wx, r_wx, 0)
        along(j, half_of(xl, core, 0), s_wf, r_wf, 0, at_r).start()
        along(j, slab_of(xl, core), s_ws, r_ws, 1, sib).start()
        wait_in(j, slab_of(xr, core), s_wx, r_wx, 1)
        along(j, half_of(xr, core, 1), s_wf, r_wf, 1, at_l).start()
        along(j, slab_of(xr, core), s_ws, r_ws, 2, sib).start()

    def stage_c(j):
        wait_in(j, half_of(xo, core, 0), s_wf, r_wf, 0)
        along(j, half_of(xo, core, 0), s_ws, r_ws, 3, sib).start()
        wait_in(j, half_of(xo, core, 1), s_wf, r_wf, 1)
        along(j, half_of(xo, core, 1), s_ws, r_ws, 4, sib).start()

    def stage_d(j):
        for item, rows in enumerate(relays(1 - core)):
            wait_in(j, rows, s_ws, r_ws, item)

    def weights_left(j):
        left(wp.at[j, here], s_w1.at[j], r_w1.at[j])
        for item in range(2):
            left(wp.at[j, here], s_wx.at[j, item], r_wx.at[j, item])
            left(wp.at[j, half_of(x, core, 0)], s_wf.at[j, item], r_wf.at[j, item])
        for item, rows in enumerate(relays(core)):
            left(wp.at[j, rows], s_ws.at[j, item], r_ws.at[j, item])

    w1(1).start()
    w1(0).start()

    for step in range(1, 2 * NX):
        i = (me + step) % (2 * NX)
        arrived(a1.at[i], s_a1.at[i], r_a1.at[i])
        arrived(p1.at[i], s_p1.at[i], r_p1.at[i])

    run = jnp.zeros((part, p1.shape[2]), F32)
    scale = jnp.ones((1, p1.shape[2]), F32)
    for i in range(2 * NX):
        xs[i] = run
        acc[i] = scale
        run = run * a1[i] + p1[i].astype(F32)
        scale = scale * a1[i]
    t_out[...] = run.astype(BF16)
    a_out[...] = scale

    for far in range(1, REACH + 1):

        @pl.when(z + far < NZ)
        def _():
            to = ctx + far * 2 * NX
            rdma(a_out, a_in.at[far - 1], s_a2.at[far - 1], r_a2.at[far - 1], to, y).start()
            rdma(t_out, t_in.at[far - 1], s_p2.at[far - 1], r_p2.at[far - 1], to, y).start()

    stage_a(1)

    plane[...] = jnp.zeros_like(plane)
    for far in range(REACH, 0, -1):

        @pl.when(z - far >= 0)
        def _():
            arrived(a_in.at[far - 1], s_a2.at[far - 1], r_a2.at[far - 1])
            arrived(t_in.at[far - 1], s_p2.at[far - 1], r_p2.at[far - 1])
            plane[...] = plane[...] * a_in[far - 1] + t_in[far - 1].astype(F32)

    for i in range(2 * NX):
        p3[i] = (xs[i] + acc[i] * plane[...]).astype(BF16)
    for step in range(1, 2 * NX):
        i = (me + step) % (2 * NX)
        rdma(p3.at[i], e_in.at[rows_of(me), :], s_p3.at[i], r_p3.at[me], base + i, y).start()
    e_in[rows_of(me), :] = p3[me]

    for load in loads[:3]:
        load.wait()
    stage_b(1)

    for step in range(1, 2 * NX):
        i = (me + step) % (2 * NX)
        arrived(e_in.at[rows_of(i), :], s_p3.at[i], r_p3.at[i])

    heads = reach.shape[1] // DK

    def chunk_rows(c):
        return pl.ds(pl.multiple_of(c * CH, CH), CH)

    def hidden_step(c, carry):
        rows = chunk_rows(c)
        for h in range(heads):
            kc = slice(h * DK, (h + 1) * DK)
            vc = slice(h * DV, (h + 1) * DV)
            full = mixed[rows, vc].astype(F32)
            full += dot(reach[rows, kc], e_in[:, kc], ((1,), (1,)))
            mean = jnp.mean(full * full, axis=-1, keepdims=True)
            val = gate[rows, vc].astype(F32)
            silu = val / (1.0 + jnp.exp(-val))
            hid[rows, vc] = (full * lax.rsqrt(mean + 1e-5) * silu).astype(BF16)
        rdma(hid.at[rows, :], hid_peer.at[rows, :], s_hid.at[c], r_hid.at[c], ctx, pair).start()
        return carry

    lax.fori_loop(0, chunks, hidden_step, 0)

    stage_c(1)
    stage_a(0)
    for load in loads[3:]:
        load.wait()
    stage_d(1)

    tile = 512

    def product(rows, j, n):
        cols = pl.ds(pl.multiple_of(n * tile, tile), tile)
        total = dot(hid[rows, :], wo[j, :, cols], ((1,), (0,)))
        return total + dot(hid_peer[rows, :], wp[j, :, cols], ((1,), (0,))), cols

    lag = 2

    def main_step(c, carry):
        @pl.when(c < chunks)
        def _():
            rows = chunk_rows(c)
            arrived(hid_peer.at[rows, :], s_hid.at[c], r_hid.at[c])

            def column(n, carry):
                total, cols = product(rows, 1, n)
                send[rows, cols] = total.astype(BF16)
                return carry

            lax.fori_loop(0, width // tile, column, 0)
            rdma(send.at[rows, :], recv.at[rows, :], s_rs.at[c], r_rs.at[c], ctx, over).start()

        @pl.when(c == 0)
        def _():
            stage_b(0)

        @pl.when(c == 1)
        def _():
            stage_c(0)

        @pl.when(c == lag)
        def _():
            stage_d(0)

        @pl.when(c >= lag)
        def _():
            d = c - lag
            rows = chunk_rows(d)

            def column(n, carry):
                total, cols = product(rows, 0, n)
                own[:, cols] = total
                return carry

            lax.fori_loop(0, width // tile, column, 0)
            arrived(recv.at[rows, :], s_rs.at[d], r_rs.at[d])
            res[rows, :] = (own[...] + recv[rows, :].astype(F32)).astype(BF16)
            pltpu.make_async_copy(res.at[rows, :], out_h.at[rows, :], s_out.at[d]).start()

        return carry

    lax.fori_loop(0, chunks + lag, main_step, 0)

    for step in range(1, 2 * NX):
        i = (me + step) % (2 * NX)
        left(decay, s_a1.at[i], r_a1.at[i])
        left(p1.at[i], s_p1.at[i], r_p1.at[i])
        left(p3.at[i], s_p3.at[i], r_p3.at[i])
    for far in range(1, REACH + 1):

        @pl.when(z + far < NZ)
        def _():
            left(a_out, s_a2.at[far - 1], r_a2.at[far - 1])
            left(t_out, s_p2.at[far - 1], r_p2.at[far - 1])

    weights_left(1)
    weights_left(0)

    def finish(c, carry):
        rows = chunk_rows(c)
        left(hid.at[rows, :], s_hid.at[c], r_hid.at[c])
        left(send.at[rows, :], s_rs.at[c], r_rs.at[c])
        pltpu.make_async_copy(res.at[rows, :], out_h.at[rows, :], s_out.at[c]).wait()
        return carry

    lax.fori_loop(0, chunks, finish, 0)


def shards(queries, keys, values, log_gate, out_gate, segment_ids, final_projector):
    tokens = queries.shape[0]
    keys_wide = queries.shape[1]
    vals_wide = values.shape[1]
    blocks = tokens // CH
    depth, full = final_projector.shape
    width = full // 4
    slots = 2 * NX
    part = DV // slots
    chunks = tokens // CH

    first_block = lax.axis_index("ctx") * blocks
    padded = jnp.concatenate([segment_ids[:1] - 1, segment_ids])
    current = lax.dynamic_slice_in_dim(padded, first_block + 1, blocks)
    before = lax.dynamic_slice_in_dim(padded, first_block, blocks)
    keep = (current == before).astype(F32)

    def by_block(wide):
        return pl.BlockSpec((CH, wide), lambda b: (b, 0))

    whole = lambda b: (0, 0)
    mixed, reach, state, decay = pl.pallas_call(
        local_kernel,
        grid=(blocks,),
        in_specs=[
            pl.BlockSpec(memory_space=pltpu.SMEM),
            by_block(keys_wide),
            by_block(keys_wide),
            by_block(vals_wide),
            by_block(keys_wide),
        ],
        out_specs=[
            by_block(vals_wide),
            by_block(keys_wide),
            pl.BlockSpec((DV, keys_wide), whole),
            pl.BlockSpec((1, keys_wide), whole),
        ],
        out_shape=[
            jax.ShapeDtypeStruct((tokens, vals_wide), BF16),
            jax.ShapeDtypeStruct((tokens, keys_wide), BF16),
            jax.ShapeDtypeStruct((DV, keys_wide), BF16),
            jax.ShapeDtypeStruct((1, keys_wide), F32),
        ],
        scratch_shapes=[pltpu.VMEM((DV, keys_wide), F32), pltpu.VMEM((1, keys_wide), F32)],
        compiler_params=pltpu.CompilerParams(vmem_limit_bytes=32 * 2**20),
    )(keep, queries, keys, values, log_gate)

    vm = pltpu.VMEM
    dma = pltpu.SemaphoreType.DMA
    return pl.pallas_call(
        exchange_kernel,
        in_specs=[pl.BlockSpec(memory_space=pltpu.VMEM)] * 2 + [pl.BlockSpec(memory_space=pl.ANY)] * 4,
        out_specs=pl.BlockSpec(memory_space=pl.ANY),
        out_shape=jax.ShapeDtypeStruct((tokens, width), BF16),
        scratch_shapes=[
            vm((tokens, vals_wide), BF16),
            vm((tokens, keys_wide), BF16),
            vm((tokens, vals_wide), BF16),
            vm((2, depth, width), BF16),
            vm((2, depth, width), BF16),
            vm((tokens, vals_wide), BF16),
            vm((tokens, vals_wide), BF16),
            vm((tokens, width), BF16),
            vm((tokens, width), BF16),
            vm((tokens, width), BF16),
            vm((CH, width), F32),
            vm((slots, part, keys_wide), BF16),
            vm((slots, 1, keys_wide), F32),
            vm((slots, part, keys_wide), F32),
            vm((slots, 1, keys_wide), F32),
            vm((part, keys_wide), BF16),
            vm((1, keys_wide), F32),
            vm((REACH, part, keys_wide), BF16),
            vm((REACH, 1, keys_wide), F32),
            vm((part, keys_wide), F32),
            vm((slots, part, keys_wide), BF16),
            vm((DV, keys_wide), BF16),
            dma((slots,)), dma((slots,)),
            dma((slots,)), dma((slots,)),
            dma((REACH,)), dma((REACH,)),
            dma((REACH,)), dma((REACH,)),
            dma((slots,)), dma((slots,)),
            dma((2,)), dma((2,)),
            dma((2, 2)), dma((2, 2)),
            dma((2, 2)), dma((2, 2)),
            dma((2, 5)), dma((2, 5)),
            dma((chunks,)), dma((chunks,)),
            dma((chunks,)), dma((chunks,)),
            dma((5,)),
            dma((chunks,)),
        ],
        compiler_params=pltpu.CompilerParams(
            collective_id=0, has_side_effects=True, vmem_limit_bytes=48 * 2**20
        ),
    )(state, decay, mixed, reach, out_gate, final_projector)


def solution(mesh):
    return jax.shard_map(
        shards,
        mesh=mesh,
        in_specs=(
            P("ctx", "head"),
            P("ctx", "head"),
            P("ctx", "head"),
            P("ctx", "head"),
            P("ctx", "head"),
            P(),
            P("head", None),
        ),
        out_specs=P("ctx", "head"),
        check_vma=False,
    )
```

```python
import jax
import jax.numpy as jnp
from jax import lax
from jax.experimental import pallas as pl
from jax.experimental.pallas import tpu as pltpu
from jax.sharding import PartitionSpec as P

DK = 128
DV = 256
CH = 128
F32 = jnp.float32
BF16 = jnp.bfloat16
MESH = pl.DeviceIdType.MESH

NX = 4
NZ = 8
PIECE = 64
REACH = 4


def dot(a, b, dims):
    return lax.dot_general(a, b, (dims, ((), ())), preferred_element_type=F32)


def layer_kernel(
    seg, g_h, k_h, v_h, q_h, gate_h, proj_h, out_h,
    g, k, v, q, cum, state_f, state, starts, weights, decay,
    mixed, reach, gate, wo, wp, hid, hid_peer, send, recv, res, own,
    p1, a1, xs, acc, t_out, a_out, t_in, a_in, plane, p3, e_in,
    s_p1, r_p1, s_a1, r_a1, s_p2, r_p2, s_a2, r_a2, s_p3, r_p3,
    s_w1, r_w1, s_wx, r_wx, s_wf, r_wf, s_ws, r_ws,
    s_hid, r_hid, s_rs, r_rs, s_load, s_out,
):
    ctx = lax.axis_index("ctx")
    y = lax.axis_index("head")
    z = ctx // (2 * NX)
    me = ctx % (2 * NX)
    x = me // 2
    core = me % 2
    base = z * (2 * NX)
    pair = y + 1 - 2 * (y % 2)
    over = 3 - y
    xr = (x + 1) % NX
    xl = (x + NX - 1) % NX
    xo = (x + 2) % NX
    tokens = hid.shape[0]
    blocks = tokens // CH
    chunks = tokens // PIECE
    heads = reach.shape[1] // DK
    width = wo.shape[2]
    depth = wo.shape[1]
    slab = depth // (2 * NX)
    part = p1.shape[1]

    def rdma(src, dst, ssem, rsem, c, h):
        return pltpu.make_async_remote_copy(
            src_ref=src, dst_ref=dst, send_sem=ssem, recv_sem=rsem,
            device_id={"ctx": c, "head": h}, device_id_type=MESH,
        )

    def arrived(dst, ssem, rsem):
        rdma(dst, dst, ssem, rsem, ctx, pair).wait_recv()

    def left(src, ssem, rsem):
        rdma(src, src, ssem, rsem, ctx, pair).wait_send()

    mine_cols = pl.ds(pl.multiple_of(y * width, width), width)
    over_cols = pl.ds(pl.multiple_of(over * width, width), width)
    loads = [
        pltpu.make_async_copy(src, dst, s_load.at[i])
        for i, (src, dst) in enumerate(
            (
                (g_h, g), (k_h, k), (v_h, v), (q_h, q), (gate_h, gate),
                (proj_h.at[:, over_cols], wo.at[1]), (proj_h.at[:, mine_cols], wo.at[0]),
            )
        )
    ]
    for load in loads:
        load.start()

    barrier = pltpu.get_barrier_semaphore()

    def greet(c, h):
        pl.semaphore_signal(barrier, inc=1, device_id={"ctx": c, "head": h}, device_id_type=MESH)

    greet(ctx, pair)
    greet(ctx, over)
    for step in range(1, 2 * NX):
        greet(base + (me + step) % (2 * NX), y)
    for far in range(1, REACH + 1):

        @pl.when(z + far < NZ)
        def _():
            greet(ctx + far * 2 * NX, y)

        @pl.when(z - far >= 0)
        def _():
            greet(ctx - far * 2 * NX, y)

    ahead = jnp.minimum(NZ - 1 - z, REACH)
    behind = jnp.minimum(z, REACH)
    pl.semaphore_wait(barrier, 2 * NX + 1 + ahead + behind)

    def slab_of(xx, cc):
        return pl.ds(pl.multiple_of((xx * 2 + cc) * slab, slab), slab)

    def half_of(xx, cc, half):
        return pl.ds(pl.multiple_of((xx * 2 + cc) * slab + half * (slab // 2), slab // 2), slab // 2)

    pair_cols = (
        pl.ds(pl.multiple_of(pair * width, width), width),
        pl.ds(pl.multiple_of((3 - pair) * width, width), width),
    )
    here = slab_of(x, core)
    at_r = base + xr * 2 + core
    at_l = base + xl * 2 + core
    sib = base + x * 2 + 1 - core

    def w1(j):
        return rdma(proj_h.at[here, pair_cols[j]], wp.at[j, here], s_w1.at[j], r_w1.at[j], ctx, pair)

    def along(j, rows, s, r, item, to):
        return rdma(wp.at[j, rows], wp.at[j, rows], s.at[j, item], r.at[j, item], to, y)

    def wait_in(j, rows, s, r, item):
        arrived(wp.at[j, rows], s.at[j, item], r.at[j, item])

    def relays(cc):
        return (
            slab_of(x, cc), slab_of(xl, cc), slab_of(xr, cc), half_of(xo, cc, 0), half_of(xo, cc, 1),
        )

    def stage_a(j):
        arrived(wp.at[j, here], s_w1.at[j], r_w1.at[j])
        along(j, here, s_wx, r_wx, 0, at_r).start()
        along(j, here, s_wx, r_wx, 1, at_l).start()
        along(j, here, s_ws, r_ws, 0, sib).start()

    def stage_b(j):
        wait_in(j, slab_of(xl, core), s_wx, r_wx, 0)
        along(j, half_of(xl, core, 0), s_wf, r_wf, 0, at_r).start()
        along(j, slab_of(xl, core), s_ws, r_ws, 1, sib).start()
        wait_in(j, slab_of(xr, core), s_wx, r_wx, 1)
        along(j, half_of(xr, core, 1), s_wf, r_wf, 1, at_l).start()
        along(j, slab_of(xr, core), s_ws, r_ws, 2, sib).start()

    def stage_c(j):
        wait_in(j, half_of(xo, core, 0), s_wf, r_wf, 0)
        along(j, half_of(xo, core, 0), s_ws, r_ws, 3, sib).start()
        wait_in(j, half_of(xo, core, 1), s_wf, r_wf, 1)
        along(j, half_of(xo, core, 1), s_ws, r_ws, 4, sib).start()

    def stage_d(j):
        for item, rows in enumerate(relays(1 - core)):
            wait_in(j, rows, s_ws, r_ws, item)

    def weights_left(j):
        left(wp.at[j, here], s_w1.at[j], r_w1.at[j])
        for item in range(2):
            left(wp.at[j, here], s_wx.at[j, item], r_wx.at[j, item])
            left(wp.at[j, half_of(x, core, 0)], s_wf.at[j, item], r_wf.at[j, item])
        for item, rows in enumerate(relays(core)):
            left(wp.at[j, rows], s_ws.at[j, item], r_ws.at[j, item])

    w1(1).start()
    w1(0).start()

    block_rows = lax.broadcasted_iota(jnp.int32, (CH, CH), 0)
    block_cols = lax.broadcasted_iota(jnp.int32, (CH, CH), 1)
    causal = block_cols <= block_rows
    ones = causal.astype(F32).astype(BF16)
    state_f[...] = jnp.zeros_like(state_f)
    decay[...] = jnp.ones_like(decay)

    def rows_at(c, size):
        return pl.ds(pl.multiple_of(c * size, size), size)

    def head_keys(h):
        return slice(h * DK, (h + 1) * DK)

    def head_vals(h):
        return slice(h * DV, (h + 1) * DV)

    for load in loads[:3]:
        load.wait()

    def state_step(b, carry):
        rows = rows_at(b, CH)
        at = ctx * blocks + b
        same = jnp.logical_and(seg[at] == seg[jnp.maximum(at - 1, 0)], at > 0)
        keep = jnp.where(same, 1.0, 0.0)
        sums = dot(ones, g[rows, :], ((1,), (0,)))
        cum[rows, :] = sums
        last = sums[CH - 1 : CH, :]
        kept = (k[rows, :].astype(F32) * jnp.exp(last - sums)).astype(BF16)
        fall = jnp.exp(last)
        weight = decay[...] * keep
        weights[b] = weight
        decay[...] = weight * fall
        for h in range(heads):
            kc = head_keys(h)
            start = state_f[:, kc] * keep
            starts[b, :, kc] = start.astype(BF16)
            state_f[:, kc] = start * fall[:, kc] + dot(v[rows, head_vals(h)], kept[:, kc], ((0,), (0,)))
        return carry

    lax.fori_loop(0, blocks, state_step, 0)
    state[...] = state_f[...].astype(BF16)

    def rows_of(i):
        return pl.ds(pl.multiple_of(i * part, part), part)

    for step in range(1, 2 * NX):
        i = (me + step) % (2 * NX)
        rdma(decay, a1.at[me], s_a1.at[i], r_a1.at[me], base + i, y).start()
        rdma(state.at[rows_of(i), :], p1.at[me], s_p1.at[i], r_p1.at[me], base + i, y).start()
    p1[me] = state[rows_of(me), :]
    a1[me] = decay[...]


    def block_step(b, carry):
        rows = rows_at(b, CH)
        sums = cum[rows, :]
        dq = q[rows, :].astype(F32) * jnp.exp(sums) * DK ** (-0.5)
        dk = (k[rows, :].astype(F32) * jnp.exp(-sums)).astype(BF16)
        reach[rows, :] = (dq * weights[b]).astype(BF16)
        dq = dq.astype(BF16)
        for h in range(heads):
            kc = head_keys(h)
            vc = head_vals(h)
            scores = dot(dq[:, kc], dk[:, kc], ((1,), (1,)))
            probs = jnp.where(causal, scores, 0.0).astype(BF16)
            out = dot(probs, v[rows, vc], ((1,), (0,)))
            out += dot(dq[:, kc], starts[b, :, kc], ((1,), (1,)))
            mixed[rows, vc] = out.astype(BF16)
        return carry

    loads[3].wait()
    lax.fori_loop(0, blocks // 2, block_step, 0)


    for step in range(1, 2 * NX):
        i = (me + step) % (2 * NX)
        arrived(a1.at[i], s_a1.at[i], r_a1.at[i])
        arrived(p1.at[i], s_p1.at[i], r_p1.at[i])

    run = jnp.zeros((part, p1.shape[2]), F32)
    scale = jnp.ones((1, p1.shape[2]), F32)
    for i in range(2 * NX):
        xs[i] = run
        acc[i] = scale
        run = run * a1[i] + p1[i].astype(F32)
        scale = scale * a1[i]
    t_out[...] = run.astype(BF16)
    a_out[...] = scale

    for far in range(1, REACH + 1):

        @pl.when(z + far < NZ)
        def _():
            to = ctx + far * 2 * NX
            rdma(a_out, a_in.at[far - 1], s_a2.at[far - 1], r_a2.at[far - 1], to, y).start()
            rdma(t_out, t_in.at[far - 1], s_p2.at[far - 1], r_p2.at[far - 1], to, y).start()

    stage_a(1)
    lax.fori_loop(blocks // 2, blocks, block_step, 0)

    plane[...] = jnp.zeros_like(plane)
    for far in range(REACH, 0, -1):

        @pl.when(z - far >= 0)
        def _():
            arrived(a_in.at[far - 1], s_a2.at[far - 1], r_a2.at[far - 1])
            arrived(t_in.at[far - 1], s_p2.at[far - 1], r_p2.at[far - 1])
            plane[...] = plane[...] * a_in[far - 1] + t_in[far - 1].astype(F32)

    for i in range(2 * NX):
        p3[i] = (xs[i] + acc[i] * plane[...]).astype(BF16)
    for step in range(1, 2 * NX):
        i = (me + step) % (2 * NX)
        rdma(p3.at[i], e_in.at[rows_of(me), :], s_p3.at[i], r_p3.at[me], base + i, y).start()
    e_in[rows_of(me), :] = p3[me]

    loads[4].wait()
    stage_b(1)

    for step in range(1, 2 * NX):
        i = (me + step) % (2 * NX)
        arrived(e_in.at[rows_of(i), :], s_p3.at[i], r_p3.at[i])

    def hidden_step(c, carry):
        rows = rows_at(c, PIECE)
        for h in range(heads):
            kc = head_keys(h)
            vc = head_vals(h)
            full = mixed[rows, vc].astype(F32)
            full += dot(reach[rows, kc], e_in[:, kc], ((1,), (1,)))
            mean = jnp.mean(full * full, axis=-1, keepdims=True)
            val = gate[rows, vc].astype(F32)
            silu = val / (1.0 + jnp.exp(-val))
            hid[rows, vc] = (full * lax.rsqrt(mean + 1e-5) * silu).astype(BF16)
        rdma(hid.at[rows, :], hid_peer.at[rows, :], s_hid.at[c], r_hid.at[c], ctx, pair).start()
        return carry

    lax.fori_loop(0, chunks, hidden_step, 0)

    stage_c(1)
    stage_a(0)
    for load in loads[5:]:
        load.wait()
    stage_d(1)

    tile = 512

    def product(rows, j, n):
        cols = pl.ds(pl.multiple_of(n * tile, tile), tile)
        total = dot(hid[rows, :], wo[j, :, cols], ((1,), (0,)))
        return total + dot(hid_peer[rows, :], wp[j, :, cols], ((1,), (0,))), cols

    lag = 2

    def main_step(c, carry):
        @pl.when(c < chunks)
        def _():
            rows = rows_at(c, PIECE)
            arrived(hid_peer.at[rows, :], s_hid.at[c], r_hid.at[c])

            def column(n, carry):
                total, cols = product(rows, 1, n)
                send[rows, cols] = total.astype(BF16)
                return carry

            lax.fori_loop(0, width // tile, column, 0)
            rdma(send.at[rows, :], recv.at[rows, :], s_rs.at[c], r_rs.at[c], ctx, over).start()

        @pl.when(c == 0)
        def _():
            stage_b(0)

        @pl.when(c == 1)
        def _():
            stage_c(0)

        @pl.when(c == lag)
        def _():
            stage_d(0)

        @pl.when(c >= lag)
        def _():
            d = c - lag
            rows = rows_at(d, PIECE)

            def column(n, carry):
                total, cols = product(rows, 0, n)
                own[:, cols] = total
                return carry

            lax.fori_loop(0, width // tile, column, 0)
            arrived(recv.at[rows, :], s_rs.at[d], r_rs.at[d])
            res[rows, :] = (own[...] + recv[rows, :].astype(F32)).astype(BF16)
            pltpu.make_async_copy(res.at[rows, :], out_h.at[rows, :], s_out.at[d]).start()

        return carry

    lax.fori_loop(0, chunks + lag, main_step, 0)

    for step in range(1, 2 * NX):
        i = (me + step) % (2 * NX)
        left(decay, s_a1.at[i], r_a1.at[i])
        left(p1.at[i], s_p1.at[i], r_p1.at[i])
        left(p3.at[i], s_p3.at[i], r_p3.at[i])
    for far in range(1, REACH + 1):

        @pl.when(z + far < NZ)
        def _():
            left(a_out, s_a2.at[far - 1], r_a2.at[far - 1])
            left(t_out, s_p2.at[far - 1], r_p2.at[far - 1])

    weights_left(1)
    weights_left(0)

    def finish(c, carry):
        rows = rows_at(c, PIECE)
        left(hid.at[rows, :], s_hid.at[c], r_hid.at[c])
        left(send.at[rows, :], s_rs.at[c], r_rs.at[c])
        pltpu.make_async_copy(res.at[rows, :], out_h.at[rows, :], s_out.at[c]).wait()
        return carry

    lax.fori_loop(0, chunks, finish, 0)


def shards(queries, keys, values, log_gate, out_gate, segment_ids, final_projector):
    tokens = queries.shape[0]
    keys_wide = queries.shape[1]
    vals_wide = values.shape[1]
    depth, full = final_projector.shape
    width = full // 4
    slots = 2 * NX
    part = DV // slots
    blocks = tokens // CH
    chunks = tokens // PIECE

    vm = pltpu.VMEM
    dma = pltpu.SemaphoreType.DMA
    return pl.pallas_call(
        layer_kernel,
        in_specs=[pl.BlockSpec(memory_space=pltpu.SMEM)] + [pl.BlockSpec(memory_space=pl.ANY)] * 6,
        out_specs=pl.BlockSpec(memory_space=pl.ANY),
        out_shape=jax.ShapeDtypeStruct((tokens, width), BF16),
        scratch_shapes=[
            vm((tokens, keys_wide), BF16),
            vm((tokens, keys_wide), BF16),
            vm((tokens, vals_wide), BF16),
            vm((tokens, keys_wide), BF16),
            vm((tokens, keys_wide), F32),
            vm((DV, keys_wide), F32),
            vm((DV, keys_wide), BF16),
            vm((blocks, DV, keys_wide), BF16),
            vm((blocks, 1, keys_wide), F32),
            vm((1, keys_wide), F32),
            vm((tokens, vals_wide), BF16),
            vm((tokens, keys_wide), BF16),
            vm((tokens, vals_wide), BF16),
            vm((2, depth, width), BF16),
            vm((2, depth, width), BF16),
            vm((tokens, vals_wide), BF16),
            vm((tokens, vals_wide), BF16),
            vm((tokens, width), BF16),
            vm((tokens, width), BF16),
            vm((tokens, width), BF16),
            vm((PIECE, width), F32),
            vm((slots, part, keys_wide), BF16),
            vm((slots, 1, keys_wide), F32),
            vm((slots, part, keys_wide), F32),
            vm((slots, 1, keys_wide), F32),
            vm((part, keys_wide), BF16),
            vm((1, keys_wide), F32),
            vm((REACH, part, keys_wide), BF16),
            vm((REACH, 1, keys_wide), F32),
            vm((part, keys_wide), F32),
            vm((slots, part, keys_wide), BF16),
            vm((DV, keys_wide), BF16),
            dma((slots,)), dma((slots,)),
            dma((slots,)), dma((slots,)),
            dma((REACH,)), dma((REACH,)),
            dma((REACH,)), dma((REACH,)),
            dma((slots,)), dma((slots,)),
            dma((2,)), dma((2,)),
            dma((2, 2)), dma((2, 2)),
            dma((2, 2)), dma((2, 2)),
            dma((2, 5)), dma((2, 5)),
            dma((chunks,)), dma((chunks,)),
            dma((chunks,)), dma((chunks,)),
            dma((7,)),
            dma((chunks,)),
        ],
        compiler_params=pltpu.CompilerParams(
            collective_id=0, has_side_effects=True, vmem_limit_bytes=56 * 2**20
        ),
    )(segment_ids, log_gate, keys, values, queries, out_gate, final_projector)


def solution(mesh):
    return jax.shard_map(
        shards,
        mesh=mesh,
        in_specs=(
            P("ctx", "head"),
            P("ctx", "head"),
            P("ctx", "head"),
            P("ctx", "head"),
            P("ctx", "head"),
            P(),
            P("head", None),
        ),
        out_specs=P("ctx", "head"),
        check_vma=False,
    )
```

```python
import jax
import jax.numpy as jnp
from jax import lax
from jax.experimental import pallas as pl
from jax.experimental.pallas import tpu as pltpu
from jax.sharding import PartitionSpec as P

DK = 128
DV = 256
CH = 128
F32 = jnp.float32
BF16 = jnp.bfloat16
MESH = pl.DeviceIdType.MESH

NX = 4
NZ = 8
PIECE = 64
REACH = 4


def dot(a, b, dims):
    return lax.dot_general(a, b, (dims, ((), ())), preferred_element_type=F32)


def layer_kernel(
    seg, g_h, k_h, v_h, q_h, gate_h, proj_h, out_h,
    g, k, v, q, cum, state_f, state, starts, weights, decay,
    mixed, reach, gate, wo, wp, hid, hid_peer, send, recv, res, own, ahead_of,
    p1, a1, xs, acc, t_out, a_out, t_in, a_in, plane, p3, e_in,
    s_p1, r_p1, s_a1, r_a1, s_p2, r_p2, s_a2, r_a2, s_p3, r_p3,
    s_w1, r_w1, s_wx, r_wx, s_wf, r_wf, s_ws, r_ws,
    s_hid, r_hid, s_rs, r_rs, s_load, s_out,
):
    ctx = lax.axis_index("ctx")
    y = lax.axis_index("head")
    z = ctx // (2 * NX)
    me = ctx % (2 * NX)
    x = me // 2
    core = me % 2
    base = z * (2 * NX)
    pair = y + 1 - 2 * (y % 2)
    over = 3 - y
    xr = (x + 1) % NX
    xl = (x + NX - 1) % NX
    xo = (x + 2) % NX
    tokens = hid.shape[0]
    blocks = tokens // CH
    chunks = tokens // PIECE
    heads = reach.shape[1] // DK
    width = wo.shape[2]
    depth = wo.shape[1]
    slab = depth // (2 * NX)
    part = p1.shape[2]

    def rdma(src, dst, ssem, rsem, c, h):
        return pltpu.make_async_remote_copy(
            src_ref=src, dst_ref=dst, send_sem=ssem, recv_sem=rsem,
            device_id={"ctx": c, "head": h}, device_id_type=MESH,
        )

    def arrived(dst, ssem, rsem):
        rdma(dst, dst, ssem, rsem, ctx, pair).wait_recv()

    def left(src, ssem, rsem):
        rdma(src, src, ssem, rsem, ctx, pair).wait_send()

    mine_cols = pl.ds(pl.multiple_of(y * width, width), width)
    over_cols = pl.ds(pl.multiple_of(over * width, width), width)
    loads = [
        pltpu.make_async_copy(src, dst, s_load.at[i])
        for i, (src, dst) in enumerate(
            (
                (g_h, g), (k_h, k), (v_h, v), (q_h, q), (gate_h, gate),
                (proj_h.at[:, over_cols], wo.at[1]), (proj_h.at[:, mine_cols], wo.at[0]),
            )
        )
    ]
    for load in loads:
        load.start()

    barrier = pltpu.get_barrier_semaphore()

    def greet(c, h):
        pl.semaphore_signal(barrier, inc=1, device_id={"ctx": c, "head": h}, device_id_type=MESH)

    greet(ctx, pair)
    greet(ctx, over)
    for step in range(1, 2 * NX):
        greet(base + (me + step) % (2 * NX), y)
    for far in range(1, REACH + 1):

        @pl.when(z + far < NZ)
        def _():
            greet(ctx + far * 2 * NX, y)

        @pl.when(z - far >= 0)
        def _():
            greet(ctx - far * 2 * NX, y)

    ahead = jnp.minimum(NZ - 1 - z, REACH)
    behind = jnp.minimum(z, REACH)
    pl.semaphore_wait(barrier, 2 * NX + 1 + ahead + behind)

    def slab_of(xx, cc):
        return pl.ds(pl.multiple_of((xx * 2 + cc) * slab, slab), slab)

    def half_of(xx, cc, half):
        return pl.ds(pl.multiple_of((xx * 2 + cc) * slab + half * (slab // 2), slab // 2), slab // 2)

    pair_cols = (
        pl.ds(pl.multiple_of(pair * width, width), width),
        pl.ds(pl.multiple_of((3 - pair) * width, width), width),
    )
    here = slab_of(x, core)
    at_r = base + xr * 2 + core
    at_l = base + xl * 2 + core
    sib = base + x * 2 + 1 - core

    def w1(j):
        return rdma(proj_h.at[here, pair_cols[j]], wp.at[j, here], s_w1.at[j], r_w1.at[j], ctx, pair)

    def along(j, rows, s, r, item, to):
        return rdma(wp.at[j, rows], wp.at[j, rows], s.at[j, item], r.at[j, item], to, y)

    def wait_in(j, rows, s, r, item):
        arrived(wp.at[j, rows], s.at[j, item], r.at[j, item])

    def relays(cc):
        return (
            slab_of(x, cc), slab_of(xl, cc), slab_of(xr, cc), half_of(xo, cc, 0), half_of(xo, cc, 1),
        )

    def stage_a(j):
        arrived(wp.at[j, here], s_w1.at[j], r_w1.at[j])
        along(j, here, s_wx, r_wx, 0, at_r).start()
        along(j, here, s_wx, r_wx, 1, at_l).start()
        along(j, here, s_ws, r_ws, 0, sib).start()

    def stage_b(j):
        wait_in(j, slab_of(xl, core), s_wx, r_wx, 0)
        along(j, half_of(xl, core, 0), s_wf, r_wf, 0, at_r).start()
        along(j, slab_of(xl, core), s_ws, r_ws, 1, sib).start()
        wait_in(j, slab_of(xr, core), s_wx, r_wx, 1)
        along(j, half_of(xr, core, 1), s_wf, r_wf, 1, at_l).start()
        along(j, slab_of(xr, core), s_ws, r_ws, 2, sib).start()

    def stage_c(j):
        wait_in(j, half_of(xo, core, 0), s_wf, r_wf, 0)
        along(j, half_of(xo, core, 0), s_ws, r_ws, 3, sib).start()
        wait_in(j, half_of(xo, core, 1), s_wf, r_wf, 1)
        along(j, half_of(xo, core, 1), s_ws, r_ws, 4, sib).start()

    def stage_d(j):
        for item, rows in enumerate(relays(1 - core)):
            wait_in(j, rows, s_ws, r_ws, item)

    def weights_left(j):
        left(wp.at[j, here], s_w1.at[j], r_w1.at[j])
        for item in range(2):
            left(wp.at[j, here], s_wx.at[j, item], r_wx.at[j, item])
            left(wp.at[j, half_of(x, core, 0)], s_wf.at[j, item], r_wf.at[j, item])
        for item, rows in enumerate(relays(core)):
            left(wp.at[j, rows], s_ws.at[j, item], r_ws.at[j, item])

    w1(1).start()
    w1(0).start()

    block_rows = lax.broadcasted_iota(jnp.int32, (CH, CH), 0)
    block_cols = lax.broadcasted_iota(jnp.int32, (CH, CH), 1)
    causal = block_cols <= block_rows
    ones = causal.astype(F32).astype(BF16)
    state_f[...] = jnp.zeros_like(state_f)
    decay[...] = jnp.ones_like(decay)
    wide = p1.shape[3]
    halves = p1.shape[0]
    group = heads // halves

    def rows_at(c, size):
        return pl.ds(pl.multiple_of(c * size, size), size)

    def head_keys(h):
        return slice(h * DK, (h + 1) * DK)

    def head_vals(h):
        return slice(h * DV, (h + 1) * DV)

    for load in loads[:3]:
        load.wait()

    def state_step(f, b):
        lanes = slice(f * wide, (f + 1) * wide)
        rows = rows_at(b, CH)
        at = ctx * blocks + b
        same = jnp.logical_and(seg[at] == seg[jnp.maximum(at - 1, 0)], at > 0)
        keep = jnp.where(same, 1.0, 0.0)
        sums = dot(ones, g[rows, lanes], ((1,), (0,)))
        cum[rows, lanes] = sums
        last = sums[CH - 1 : CH, :]
        kept = (k[rows, lanes].astype(F32) * jnp.exp(last - sums)).astype(BF16)
        fall = jnp.exp(last)
        weight = decay[f] * keep
        weights[b, :, lanes] = weight
        decay[f] = weight * fall
        for i in range(group):
            kc = head_keys(i)
            start = state_f[f, :, kc] * keep
            starts[b, :, head_keys(f * group + i)] = start.astype(BF16)
            added = dot(v[rows, head_vals(f * group + i)], kept[:, kc], ((0,), (0,)))
            state_f[f, :, kc] = start * fall[:, kc] + added

    def rows_of(i):
        return pl.ds(pl.multiple_of(i * part, part), part)

    for f in range(halves):

        def step_of(b, carry):
            state_step(f, b)
            return carry

        lax.fori_loop(0, blocks, step_of, 0)
        state[f] = state_f[f].astype(BF16)
        for step in range(1, 2 * NX):
            i = (me + step) % (2 * NX)
            rdma(decay.at[f], a1.at[f, me], s_a1.at[f, i], r_a1.at[f, me], base + i, y).start()
            rdma(
                state.at[f, rows_of(i), :], p1.at[f, me], s_p1.at[f, i], r_p1.at[f, me], base + i, y
            ).start()
        p1[f, me] = state[f, rows_of(me), :]
        a1[f, me] = decay[f]

    def block_step(b, carry):
        rows = rows_at(b, CH)
        sums = cum[rows, :]
        dq = q[rows, :].astype(F32) * jnp.exp(sums) * DK ** (-0.5)
        dk = (k[rows, :].astype(F32) * jnp.exp(-sums)).astype(BF16)
        reach[rows, :] = (dq * weights[b]).astype(BF16)
        dq = dq.astype(BF16)
        for h in range(heads):
            kc = head_keys(h)
            vc = head_vals(h)
            scores = dot(dq[:, kc], dk[:, kc], ((1,), (1,)))
            probs = jnp.where(causal, scores, 0.0).astype(BF16)
            out = dot(probs, v[rows, vc], ((1,), (0,)))
            out += dot(dq[:, kc], starts[b, :, kc], ((1,), (1,)))
            mixed[rows, vc] = out.astype(BF16)
        return carry

    loads[3].wait()
    lax.fori_loop(0, blocks // 2, block_step, 0)


    for f in range(halves):
        for step in range(1, 2 * NX):
            i = (me + step) % (2 * NX)
            arrived(a1.at[f, i], s_a1.at[f, i], r_a1.at[f, i])
            arrived(p1.at[f, i], s_p1.at[f, i], r_p1.at[f, i])
        run = jnp.zeros((part, wide), F32)
        scale = jnp.ones((1, wide), F32)
        for i in range(2 * NX):
            xs[f, i] = run
            acc[f, i] = scale
            run = run * a1[f, i] + p1[f, i].astype(F32)
            scale = scale * a1[f, i]
        t_out[f] = run.astype(BF16)
        a_out[f] = scale
        for far in range(1, REACH + 1):

            @pl.when(z + far < NZ)
            def _():
                to = ctx + far * 2 * NX
                n = far - 1
                rdma(a_out.at[f], a_in.at[f, n], s_a2.at[f, n], r_a2.at[f, n], to, y).start()
                rdma(t_out.at[f], t_in.at[f, n], s_p2.at[f, n], r_p2.at[f, n], to, y).start()

    stage_a(1)
    lax.fori_loop(blocks // 2, blocks, block_step, 0)

    for f in range(halves):
        plane[...] = jnp.zeros_like(plane)
        for far in range(REACH, 0, -1):

            @pl.when(z - far >= 0)
            def _():
                n = far - 1
                arrived(a_in.at[f, n], s_a2.at[f, n], r_a2.at[f, n])
                arrived(t_in.at[f, n], s_p2.at[f, n], r_p2.at[f, n])
                plane[...] = plane[...] * a_in[f, n] + t_in[f, n].astype(F32)

        for i in range(2 * NX):
            p3[f, i] = (xs[f, i] + acc[f, i] * plane[...]).astype(BF16)
        for step in range(1, 2 * NX):
            i = (me + step) % (2 * NX)
            rdma(
                p3.at[f, i], e_in.at[f, rows_of(me), :], s_p3.at[f, i], r_p3.at[f, me], base + i, y
            ).start()
        e_in[f, rows_of(me), :] = p3[f, me]

    loads[4].wait()
    stage_b(1)

    for f in range(halves):
        for step in range(1, 2 * NX):
            i = (me + step) % (2 * NX)
            arrived(e_in.at[f, rows_of(i), :], s_p3.at[f, i], r_p3.at[f, i])

    def hidden_step(c, carry):
        rows = rows_at(c, PIECE)
        for h in range(heads):
            kc = head_keys(h)
            vc = head_vals(h)
            full = mixed[rows, vc].astype(F32)
            full += dot(reach[rows, kc], e_in[h // group, :, head_keys(h % group)], ((1,), (1,)))
            mean = jnp.mean(full * full, axis=-1, keepdims=True)
            val = gate[rows, vc].astype(F32)
            silu = val / (1.0 + jnp.exp(-val))
            hid[rows, vc] = (full * lax.rsqrt(mean + 1e-5) * silu).astype(BF16)
        rdma(hid.at[rows, :], hid_peer.at[rows, :], s_hid.at[c], r_hid.at[c], ctx, pair).start()
        return carry

    lax.fori_loop(0, chunks, hidden_step, 0)

    stage_c(1)
    stage_a(0)
    for load in loads[5:]:
        load.wait()
    stage_d(1)

    tile = 512

    def columns(do):
        def column(n, carry):
            do(pl.ds(pl.multiple_of(n * tile, tile), tile))
            return carry

        lax.fori_loop(0, width // tile, column, 0)

    lag = 8
    pieces = CH // PIECE

    def main_step(c, carry):
        @pl.when(c < chunks)
        def _():
            rows = rows_at(c, PIECE)

            def own_part(cols):
                ahead_of[:, cols] = dot(hid[rows, :], wo[1, :, cols], ((1,), (0,)))

            def pair_part(cols):
                total = ahead_of[:, cols] + dot(hid_peer[rows, :], wp[1, :, cols], ((1,), (0,)))
                send[rows, cols] = total.astype(BF16)

            columns(own_part)
            arrived(hid_peer.at[rows, :], s_hid.at[c], r_hid.at[c])
            columns(pair_part)
            rdma(send.at[rows, :], recv.at[rows, :], s_rs.at[c], r_rs.at[c], ctx, over).start()

        @pl.when(c == 3)
        def _():
            stage_b(0)

        @pl.when(c == 5)
        def _():
            stage_c(0)

        @pl.when(c == lag)
        def _():
            stage_d(0)

        @pl.when(c >= lag)
        def _():
            d = c - lag
            rows = rows_at(d, CH)

            def both_parts(cols):
                total = dot(hid[rows, :], wo[0, :, cols], ((1,), (0,)))
                own[:, cols] = total + dot(hid_peer[rows, :], wp[0, :, cols], ((1,), (0,)))

            columns(both_parts)
            for piece in range(pieces):
                got = rows_at(d * pieces + piece, PIECE)
                n = d * pieces + piece
                arrived(recv.at[got, :], s_rs.at[n], r_rs.at[n])
            res[rows, :] = (own[...] + recv[rows, :].astype(F32)).astype(BF16)
            pltpu.make_async_copy(res.at[rows, :], out_h.at[rows, :], s_out.at[d]).start()

        return carry

    lax.fori_loop(0, lag + blocks, main_step, 0)

    for f in range(halves):
        for step in range(1, 2 * NX):
            i = (me + step) % (2 * NX)
            left(decay.at[f], s_a1.at[f, i], r_a1.at[f, i])
            left(p1.at[f, i], s_p1.at[f, i], r_p1.at[f, i])
            left(p3.at[f, i], s_p3.at[f, i], r_p3.at[f, i])
        for far in range(1, REACH + 1):

            @pl.when(z + far < NZ)
            def _():
                n = far - 1
                left(a_out.at[f], s_a2.at[f, n], r_a2.at[f, n])
                left(t_out.at[f], s_p2.at[f, n], r_p2.at[f, n])

    weights_left(1)
    weights_left(0)

    def finish(c, carry):
        rows = rows_at(c, PIECE)
        left(hid.at[rows, :], s_hid.at[c], r_hid.at[c])
        left(send.at[rows, :], s_rs.at[c], r_rs.at[c])
        return carry

    lax.fori_loop(0, chunks, finish, 0)
    for d in range(blocks):
        rows = rows_at(d, CH)
        pltpu.make_async_copy(res.at[rows, :], out_h.at[rows, :], s_out.at[d]).wait()


def shards(queries, keys, values, log_gate, out_gate, segment_ids, final_projector):
    tokens = queries.shape[0]
    keys_wide = queries.shape[1]
    vals_wide = values.shape[1]
    depth, full = final_projector.shape
    width = full // 4
    slots = 2 * NX
    part = DV // slots
    blocks = tokens // CH
    chunks = tokens // PIECE
    halves = 2
    wide = keys_wide // halves

    vm = pltpu.VMEM
    dma = pltpu.SemaphoreType.DMA
    return pl.pallas_call(
        layer_kernel,
        in_specs=[pl.BlockSpec(memory_space=pltpu.SMEM)] + [pl.BlockSpec(memory_space=pl.ANY)] * 6,
        out_specs=pl.BlockSpec(memory_space=pl.ANY),
        out_shape=jax.ShapeDtypeStruct((tokens, width), BF16),
        scratch_shapes=[
            vm((tokens, keys_wide), BF16),
            vm((tokens, keys_wide), BF16),
            vm((tokens, vals_wide), BF16),
            vm((tokens, keys_wide), BF16),
            vm((tokens, keys_wide), F32),
            vm((halves, DV, wide), F32),
            vm((halves, DV, wide), BF16),
            vm((blocks, DV, keys_wide), BF16),
            vm((blocks, 1, keys_wide), F32),
            vm((halves, 1, wide), F32),
            vm((tokens, vals_wide), BF16),
            vm((tokens, keys_wide), BF16),
            vm((tokens, vals_wide), BF16),
            vm((2, depth, width), BF16),
            vm((2, depth, width), BF16),
            vm((tokens, vals_wide), BF16),
            vm((tokens, vals_wide), BF16),
            vm((tokens, width), BF16),
            vm((tokens, width), BF16),
            vm((tokens, width), BF16),
            vm((CH, width), F32),
            vm((PIECE, width), F32),
            vm((halves, slots, part, wide), BF16),
            vm((halves, slots, 1, wide), F32),
            vm((halves, slots, part, wide), F32),
            vm((halves, slots, 1, wide), F32),
            vm((halves, part, wide), BF16),
            vm((halves, 1, wide), F32),
            vm((halves, REACH, part, wide), BF16),
            vm((halves, REACH, 1, wide), F32),
            vm((part, wide), F32),
            vm((halves, slots, part, wide), BF16),
            vm((halves, DV, wide), BF16),
            dma((halves, slots)), dma((halves, slots)),
            dma((halves, slots)), dma((halves, slots)),
            dma((halves, REACH)), dma((halves, REACH)),
            dma((halves, REACH)), dma((halves, REACH)),
            dma((halves, slots)), dma((halves, slots)),
            dma((2,)), dma((2,)),
            dma((2, 2)), dma((2, 2)),
            dma((2, 2)), dma((2, 2)),
            dma((2, 5)), dma((2, 5)),
            dma((chunks,)), dma((chunks,)),
            dma((chunks,)), dma((chunks,)),
            dma((7,)),
            dma((blocks,)),
        ],
        compiler_params=pltpu.CompilerParams(
            collective_id=0, has_side_effects=True, vmem_limit_bytes=56 * 2**20
        ),
    )(segment_ids, log_gate, keys, values, queries, out_gate, final_projector)


def solution(mesh):
    return jax.shard_map(
        shards,
        mesh=mesh,
        in_specs=(
            P("ctx", "head"),
            P("ctx", "head"),
            P("ctx", "head"),
            P("ctx", "head"),
            P("ctx", "head"),
            P(),
            P("head", None),
        ),
        out_specs=P("ctx", "head"),
        check_vma=False,
    )
```

```python
import jax
import jax.numpy as jnp
from jax import lax
from jax.experimental import pallas as pl
from jax.experimental.pallas import tpu as pltpu
from jax.sharding import PartitionSpec as P

DK = 128
DV = 256
CH = 128
F32 = jnp.float32
BF16 = jnp.bfloat16
MESH = pl.DeviceIdType.MESH

NX = 4
NZ = 8
PIECE = 64
CROSS = 2
REACH = 4


def dot(a, b, dims):
    return lax.dot_general(a, b, (dims, ((), ())), preferred_element_type=F32)


def layer_kernel(
    seg, g_h, k_h, v_h, q_h, gate_h, proj_h, out_h,
    g, k, v, q, cum, state_f, state, starts, weights, decay,
    mixed, reach, gate, wo, wp, hid, hid_peer, send, recv, res, own, ahead_of,
    p1, a1, xs, acc, t_out, a_out, t_in, a_in, plane, p3, e_in,
    s_p1, r_p1, s_a1, r_a1, s_p2, r_p2, s_a2, r_a2, s_p3, r_p3,
    s_w1, r_w1, s_wx, r_wx, s_wf, r_wf, s_ws, r_ws,
    s_hid, r_hid, s_rs, r_rs, s_load, s_out,
):
    ctx = lax.axis_index("ctx")
    y = lax.axis_index("head")
    z = ctx // (2 * NX)
    me = ctx % (2 * NX)
    x = me // 2
    core = me % 2
    base = z * (2 * NX)
    pair = y + 1 - 2 * (y % 2)
    over = 3 - y
    over_pair = over + 1 - 2 * (over % 2)
    xr = (x + 1) % NX
    xl = (x + NX - 1) % NX
    xo = (x + 2) % NX
    tokens = hid.shape[0]
    blocks = tokens // CH
    chunks = tokens // PIECE
    heads = reach.shape[1] // DK
    width = wo.shape[2]
    depth = wo.shape[1]
    slab = depth // (2 * NX)
    part = p1.shape[2]

    def rdma(src, dst, ssem, rsem, c, h):
        return pltpu.make_async_remote_copy(
            src_ref=src, dst_ref=dst, send_sem=ssem, recv_sem=rsem,
            device_id={"ctx": c, "head": h}, device_id_type=MESH,
        )

    def arrived(dst, ssem, rsem):
        rdma(dst, dst, ssem, rsem, ctx, pair).wait_recv()

    def left(src, ssem, rsem):
        rdma(src, src, ssem, rsem, ctx, pair).wait_send()

    mine_cols = pl.ds(pl.multiple_of(y * width, width), width)
    over_cols = pl.ds(pl.multiple_of(over * width, width), width)
    pair_cols = pl.ds(pl.multiple_of(pair * width, width), width)
    loads = [
        pltpu.make_async_copy(src, dst, s_load.at[i])
        for i, (src, dst) in enumerate(
            (
                (g_h, g), (k_h, k), (v_h, v), (q_h, q), (gate_h, gate),
                (proj_h.at[:, over_cols], wo.at[1]), (proj_h.at[:, mine_cols], wo.at[0]),
                (proj_h.at[:, pair_cols], wo.at[2]),
            )
        )
    ]
    for load in loads:
        load.start()

    barrier = pltpu.get_barrier_semaphore()

    def greet(c, h):
        pl.semaphore_signal(barrier, inc=1, device_id={"ctx": c, "head": h}, device_id_type=MESH)

    greet(ctx, pair)
    greet(ctx, over)
    for step in range(1, 2 * NX):
        greet(base + (me + step) % (2 * NX), y)
    for far in range(1, REACH + 1):

        @pl.when(z + far < NZ)
        def _():
            greet(ctx + far * 2 * NX, y)

        @pl.when(z - far >= 0)
        def _():
            greet(ctx - far * 2 * NX, y)

    ahead = jnp.minimum(NZ - 1 - z, REACH)
    behind = jnp.minimum(z, REACH)
    pl.semaphore_wait(barrier, 2 * NX + 1 + ahead + behind)

    units = (
        (1, 0, slab // 2, pair, 3 - pair),
        (1, slab // 2, slab // 2, pair, 3 - pair),
        (0, 0, slab, pair, pair),
        (3, 0, slab, over, over_pair),
        (2, 0, slab, over, over),
    )

    def unit_rows(u, xx, cc, half=None):
        _, first, size, _, _ = units[u]
        if half is not None:
            size = size // 2
            first = first + half * size
        return pl.ds(pl.multiple_of((xx * 2 + cc) * slab + first, size), size)

    at_r = base + xr * 2 + core
    at_l = base + xl * 2 + core
    sib = base + x * 2 + 1 - core

    def w1(u):
        j, _, _, to, block = units[u]
        rows = unit_rows(u, x, core)
        cols = pl.ds(pl.multiple_of(block * width, width), width)
        return rdma(proj_h.at[rows, cols], wp.at[j, rows], s_w1.at[u], r_w1.at[u], ctx, to)

    def along(u, rows, s, r, item, to):
        j = units[u][0]
        return rdma(wp.at[j, rows], wp.at[j, rows], s.at[u, item], r.at[u, item], to, y)

    def wait_in(u, rows, s, r, item):
        arrived(wp.at[units[u][0], rows], s.at[u, item], r.at[u, item])

    def relays(u, cc):
        return (
            unit_rows(u, x, cc), unit_rows(u, xl, cc), unit_rows(u, xr, cc),
            unit_rows(u, xo, cc, 0), unit_rows(u, xo, cc, 1),
        )

    def stage_a(u):
        here = unit_rows(u, x, core)
        arrived(wp.at[units[u][0], here], s_w1.at[u], r_w1.at[u])
        along(u, here, s_wx, r_wx, 0, at_r).start()
        along(u, here, s_wx, r_wx, 1, at_l).start()
        along(u, here, s_ws, r_ws, 0, sib).start()

    def stage_b(u):
        wait_in(u, unit_rows(u, xl, core), s_wx, r_wx, 0)
        along(u, unit_rows(u, xl, core, 0), s_wf, r_wf, 0, at_r).start()
        along(u, unit_rows(u, xl, core), s_ws, r_ws, 1, sib).start()
        wait_in(u, unit_rows(u, xr, core), s_wx, r_wx, 1)
        along(u, unit_rows(u, xr, core, 1), s_wf, r_wf, 1, at_l).start()
        along(u, unit_rows(u, xr, core), s_ws, r_ws, 2, sib).start()

    def stage_c(u):
        wait_in(u, unit_rows(u, xo, core, 0), s_wf, r_wf, 0)
        along(u, unit_rows(u, xo, core, 0), s_ws, r_ws, 3, sib).start()
        wait_in(u, unit_rows(u, xo, core, 1), s_wf, r_wf, 1)
        along(u, unit_rows(u, xo, core, 1), s_ws, r_ws, 4, sib).start()

    def stage_d(u):
        for item, rows in enumerate(relays(u, 1 - core)):
            wait_in(u, rows, s_ws, r_ws, item)

    def weights_left(u):
        j = units[u][0]
        here = unit_rows(u, x, core)
        left(wp.at[j, here], s_w1.at[u], r_w1.at[u])
        for item in range(2):
            left(wp.at[j, here], s_wx.at[u, item], r_wx.at[u, item])
            left(wp.at[j, unit_rows(u, x, core, 0)], s_wf.at[u, item], r_wf.at[u, item])
        for item, rows in enumerate(relays(u, core)):
            left(wp.at[j, rows], s_ws.at[u, item], r_ws.at[u, item])

    for u in (0, 1, 3, 4):
        w1(u).start()

    block_rows = lax.broadcasted_iota(jnp.int32, (CH, CH), 0)
    block_cols = lax.broadcasted_iota(jnp.int32, (CH, CH), 1)
    causal = block_cols <= block_rows
    ones = causal.astype(F32).astype(BF16)
    state_f[...] = jnp.zeros_like(state_f)
    decay[...] = jnp.ones_like(decay)
    wide = p1.shape[3]
    halves = p1.shape[0]
    group = heads // halves

    def rows_at(c, size):
        return pl.ds(pl.multiple_of(c * size, size), size)

    def head_keys(h):
        return slice(h * DK, (h + 1) * DK)

    def head_vals(h):
        return slice(h * DV, (h + 1) * DV)

    for load in loads[:3]:
        load.wait()

    def state_step(f, b):
        lanes = slice(f * wide, (f + 1) * wide)
        rows = rows_at(b, CH)
        at = ctx * blocks + b
        same = jnp.logical_and(seg[at] == seg[jnp.maximum(at - 1, 0)], at > 0)
        keep = jnp.where(same, 1.0, 0.0)
        sums = dot(ones, g[rows, lanes], ((1,), (0,)))
        cum[rows, lanes] = sums
        last = sums[CH - 1 : CH, :]
        kept = (k[rows, lanes].astype(F32) * jnp.exp(last - sums)).astype(BF16)
        fall = jnp.exp(last)
        weight = decay[f] * keep
        weights[b, :, lanes] = weight
        decay[f] = weight * fall
        for i in range(group):
            kc = head_keys(i)
            start = state_f[f, :, kc] * keep
            starts[b, :, head_keys(f * group + i)] = start.astype(BF16)
            added = dot(v[rows, head_vals(f * group + i)], kept[:, kc], ((0,), (0,)))
            state_f[f, :, kc] = start * fall[:, kc] + added

    def rows_of(i):
        return pl.ds(pl.multiple_of(i * part, part), part)

    for f in range(halves):

        def step_of(b, carry):
            state_step(f, b)
            return carry

        lax.fori_loop(0, blocks, step_of, 0, unroll=8)
        state[f] = state_f[f].astype(BF16)
        for step in range(1, 2 * NX):
            i = (me + step) % (2 * NX)
            rdma(decay.at[f], a1.at[f, me], s_a1.at[f, i], r_a1.at[f, me], base + i, y).start()
            rdma(
                state.at[f, rows_of(i), :], p1.at[f, me], s_p1.at[f, i], r_p1.at[f, me], base + i, y
            ).start()
        p1[f, me] = state[f, rows_of(me), :]
        a1[f, me] = decay[f]

    def block_step(b, carry):
        rows = rows_at(b, CH)
        sums = cum[rows, :]
        dq = q[rows, :].astype(F32) * jnp.exp(sums) * DK ** (-0.5)
        dk = (k[rows, :].astype(F32) * jnp.exp(-sums)).astype(BF16)
        reach[rows, :] = (dq * weights[b]).astype(BF16)
        dq = dq.astype(BF16)
        for h in range(heads):
            kc = head_keys(h)
            vc = head_vals(h)
            scores = dot(dq[:, kc], dk[:, kc], ((1,), (1,)))
            probs = jnp.where(causal, scores, 0.0).astype(BF16)
            out = dot(probs, v[rows, vc], ((1,), (0,)))
            out += dot(dq[:, kc], starts[b, :, kc], ((1,), (1,)))
            mixed[rows, vc] = out.astype(BF16)
        return carry

    loads[3].wait()
    first_part = 3
    lax.fori_loop(0, first_part, block_step, 0, unroll=first_part)


    stage_a(0)

    for f in range(halves):
        for step in range(1, 2 * NX):
            i = (me + step) % (2 * NX)
            arrived(a1.at[f, i], s_a1.at[f, i], r_a1.at[f, i])
            arrived(p1.at[f, i], s_p1.at[f, i], r_p1.at[f, i])
        run = jnp.zeros((part, wide), F32)
        scale = jnp.ones((1, wide), F32)
        for i in range(2 * NX):
            xs[f, i] = run
            acc[f, i] = scale
            run = run * a1[f, i] + p1[f, i].astype(F32)
            scale = scale * a1[f, i]
        t_out[f] = run.astype(BF16)
        a_out[f] = scale
        for far in range(1, REACH + 1):

            @pl.when(z + far < NZ)
            def _():
                to = ctx + far * 2 * NX
                n = far - 1
                rdma(a_out.at[f], a_in.at[f, n], s_a2.at[f, n], r_a2.at[f, n], to, y).start()
                rdma(t_out.at[f], t_in.at[f, n], s_p2.at[f, n], r_p2.at[f, n], to, y).start()

        if f == 0:
            stage_a(1)
            w1(2).start()

    lax.fori_loop(first_part, blocks, block_step, 0, unroll=blocks - first_part)
    stage_b(0)

    for f in range(halves):
        plane[...] = jnp.zeros_like(plane)
        for far in range(REACH, 0, -1):

            @pl.when(z - far >= 0)
            def _():
                n = far - 1
                arrived(a_in.at[f, n], s_a2.at[f, n], r_a2.at[f, n])
                arrived(t_in.at[f, n], s_p2.at[f, n], r_p2.at[f, n])
                plane[...] = plane[...] * a_in[f, n] + t_in[f, n].astype(F32)

        for i in range(2 * NX):
            p3[f, i] = (xs[f, i] + acc[f, i] * plane[...]).astype(BF16)
        for step in range(1, 2 * NX):
            i = (me + step) % (2 * NX)
            rdma(
                p3.at[f, i], e_in.at[f, rows_of(me), :], s_p3.at[f, i], r_p3.at[f, me], base + i, y
            ).start()
        e_in[f, rows_of(me), :] = p3[f, me]

    stage_b(1)
    loads[4].wait()
    stage_c(0)

    for f in range(halves):
        for step in range(1, 2 * NX):
            i = (me + step) % (2 * NX)
            arrived(e_in.at[f, rows_of(i), :], s_p3.at[f, i], r_p3.at[f, i])

    straight = chunks - CROSS

    def hidden_step(step, carry):
        c = jnp.where(step < 2 * CROSS, step // 2 + (step % 2) * straight, step - CROSS)
        to = jnp.where(c < straight, pair, over)
        rows = rows_at(c, PIECE)
        for h in range(heads):
            kc = head_keys(h)
            vc = head_vals(h)
            full = mixed[rows, vc].astype(F32)
            full += dot(reach[rows, kc], e_in[h // group, :, head_keys(h % group)], ((1,), (1,)))
            mean = jnp.mean(full * full, axis=-1, keepdims=True)
            val = gate[rows, vc].astype(F32)
            silu = val / (1.0 + jnp.exp(-val))
            hid[rows, vc] = (full * lax.rsqrt(mean + 1e-5) * silu).astype(BF16)
        rdma(hid.at[rows, :], hid_peer.at[rows, :], s_hid.at[c], r_hid.at[c], ctx, to).start()
        return carry

    lax.fori_loop(0, chunks, hidden_step, 0)

    stage_c(1)
    stage_a(2)
    for load in loads[5:]:
        load.wait()
    stage_d(0)
    stage_d(1)

    tile = 512

    def columns(do):
        def column(n, carry):
            do(pl.ds(pl.multiple_of(n * tile, tile), tile))
            return carry

        lax.fori_loop(0, width // tile, column, 0)

    def own_sums(first, count, j):
        rows = pl.ds(first * PIECE, count * PIECE)

        def both_parts(cols):
            total = dot(hid[rows, :], wo[0, :, cols], ((1,), (0,)))
            own[rows, cols] = total + dot(hid_peer[rows, :], wp[j, :, cols], ((1,), (0,)))

        columns(both_parts)

    def piece_at(step):
        late = step - (chunks - 2 * CROSS + 1)
        crossed = jnp.logical_and(late >= 0, late % 2 == 0)
        behind_cross = step - (late + 1) // 2
        return jnp.where(late < 0, step, jnp.where(crossed, straight + late // 2, behind_cross))

    def main_step(step, carry):
        c = piece_at(step)
        crossed = c >= straight
        to = jnp.where(crossed, pair, over)
        jo = jnp.where(crossed, 2, 1)
        jp = jnp.where(crossed, 3, 1)
        rows = rows_at(c, PIECE)

        def own_part(cols):
            ahead_of[:, cols] = dot(hid[rows, :], wo[jo, :, cols], ((1,), (0,)))

        def pair_part(cols):
            total = ahead_of[:, cols] + dot(hid_peer[rows, :], wp[jp, :, cols], ((1,), (0,)))
            send[rows, cols] = total.astype(BF16)

        columns(own_part)
        arrived(hid_peer.at[rows, :], s_hid.at[c], r_hid.at[c])
        columns(pair_part)
        rdma(send.at[rows, :], recv.at[rows, :], s_rs.at[c], r_rs.at[c], ctx, to).start()

        def at(when, *actions):
            @pl.when(step == when)
            def _():
                for action, *args in actions:
                    action(*args)

        at(3, (stage_b, 2), (stage_a, 3))
        at(5, (stage_c, 2))
        at(6, (stage_b, 3), (stage_a, 4))
        at(7, (stage_d, 2), (own_sums, 0, 4, 0))
        at(8, (stage_c, 3))
        at(9, (stage_b, 4), (own_sums, 4, 4, 0))
        at(10, (stage_d, 3))
        at(11, (stage_c, 4), (own_sums, 8, 4, 0))
        return carry

    lax.fori_loop(0, chunks, main_step, 0)
    stage_d(4)
    own_sums(12, straight - 12, 0)
    own_sums(straight, CROSS, 2)

    def result_step(step, carry):
        c = piece_at(step)
        rows = rows_at(c, PIECE)
        arrived(recv.at[rows, :], s_rs.at[c], r_rs.at[c])
        res[rows, :] = (own[rows, :] + recv[rows, :].astype(F32)).astype(BF16)
        pltpu.make_async_copy(res.at[rows, :], out_h.at[rows, :], s_out.at[c]).start()
        return carry

    lax.fori_loop(0, chunks, result_step, 0)

    for f in range(halves):
        for step in range(1, 2 * NX):
            i = (me + step) % (2 * NX)
            left(decay.at[f], s_a1.at[f, i], r_a1.at[f, i])
            left(p1.at[f, i], s_p1.at[f, i], r_p1.at[f, i])
            left(p3.at[f, i], s_p3.at[f, i], r_p3.at[f, i])
        for far in range(1, REACH + 1):

            @pl.when(z + far < NZ)
            def _():
                n = far - 1
                left(a_out.at[f], s_a2.at[f, n], r_a2.at[f, n])
                left(t_out.at[f], s_p2.at[f, n], r_p2.at[f, n])

    for u in range(len(units)):
        weights_left(u)

    def finish(c, carry):
        rows = rows_at(c, PIECE)
        left(hid.at[rows, :], s_hid.at[c], r_hid.at[c])
        left(send.at[rows, :], s_rs.at[c], r_rs.at[c])
        pltpu.make_async_copy(res.at[rows, :], out_h.at[rows, :], s_out.at[c]).wait()
        return carry

    lax.fori_loop(0, chunks, finish, 0)


def copy_kernel(src, dst, held, s_in, s_out):
    parts = s_in.shape[0]
    size = src.shape[0] // parts
    reads = [
        pltpu.make_async_copy(src.at[pl.ds(i * size, size)], held.at[pl.ds(i * size, size)], s_in.at[i])
        for i in range(parts)
    ]
    writes = [
        pltpu.make_async_copy(held.at[pl.ds(i * size, size)], dst.at[pl.ds(i * size, size)], s_out.at[i])
        for i in range(parts)
    ]
    for read in reads:
        read.start()
    for read, write in zip(reads, writes, strict=True):
        read.wait()
        write.start()
    for write in writes:
        write.wait()


def shards(queries, keys, values, log_gate, out_gate, segment_ids, final_projector):
    tokens = queries.shape[0]
    keys_wide = queries.shape[1]
    vals_wide = values.shape[1]
    depth, full = final_projector.shape
    width = full // 4
    slots = 2 * NX
    part = DV // slots
    blocks = tokens // CH
    chunks = tokens // PIECE
    halves = 2
    wide = keys_wide // halves

    vm = pltpu.VMEM
    dma = pltpu.SemaphoreType.DMA
    projected = pl.pallas_call(
        layer_kernel,
        in_specs=[pl.BlockSpec(memory_space=pltpu.SMEM)] + [pl.BlockSpec(memory_space=pl.ANY)] * 6,
        out_specs=pl.BlockSpec(memory_space=pl.ANY),
        out_shape=jax.ShapeDtypeStruct((tokens, width), BF16),
        scratch_shapes=[
            vm((tokens, keys_wide), BF16),
            vm((tokens, keys_wide), BF16),
            vm((tokens, vals_wide), BF16),
            vm((tokens, keys_wide), BF16),
            vm((tokens, keys_wide), F32),
            vm((halves, DV, wide), F32),
            vm((halves, DV, wide), BF16),
            vm((blocks, DV, keys_wide), BF16),
            vm((blocks, 1, keys_wide), F32),
            vm((halves, 1, wide), F32),
            vm((tokens, vals_wide), BF16),
            vm((tokens, keys_wide), BF16),
            vm((tokens, vals_wide), BF16),
            vm((3, depth, width), BF16),
            vm((4, depth, width), BF16),
            vm((tokens, vals_wide), BF16),
            vm((tokens, vals_wide), BF16),
            vm((tokens, width), BF16),
            vm((tokens, width), BF16),
            vm((tokens, width), BF16),
            vm((tokens, width), F32),
            vm((PIECE, width), F32),
            vm((halves, slots, part, wide), BF16),
            vm((halves, slots, 1, wide), F32),
            vm((halves, slots, part, wide), F32),
            vm((halves, slots, 1, wide), F32),
            vm((halves, part, wide), BF16),
            vm((halves, 1, wide), F32),
            vm((halves, REACH, part, wide), BF16),
            vm((halves, REACH, 1, wide), F32),
            vm((part, wide), F32),
            vm((halves, slots, part, wide), BF16),
            vm((halves, DV, wide), BF16),
            dma((halves, slots)), dma((halves, slots)),
            dma((halves, slots)), dma((halves, slots)),
            dma((halves, REACH)), dma((halves, REACH)),
            dma((halves, REACH)), dma((halves, REACH)),
            dma((halves, slots)), dma((halves, slots)),
            dma((5,)), dma((5,)),
            dma((5, 2)), dma((5, 2)),
            dma((5, 2)), dma((5, 2)),
            dma((5, 5)), dma((5, 5)),
            dma((chunks,)), dma((chunks,)),
            dma((chunks,)), dma((chunks,)),
            dma((8,)),
            dma((chunks,)),
        ],
        compiler_params=pltpu.CompilerParams(
            collective_id=0, has_side_effects=True, vmem_limit_bytes=58 * 2**20
        ),
    )(segment_ids, log_gate, keys, values, queries, out_gate, final_projector)
    return pl.pallas_call(
        copy_kernel,
        in_specs=[pl.BlockSpec(memory_space=pl.ANY)],
        out_specs=pl.BlockSpec(memory_space=pl.ANY),
        out_shape=jax.ShapeDtypeStruct((tokens, width), BF16),
        scratch_shapes=[vm((tokens, width), BF16), dma((4,)), dma((4,))],
        compiler_params=pltpu.CompilerParams(vmem_limit_bytes=60 * 2**20),
    )(projected)


def solution(mesh):
    return jax.shard_map(
        shards,
        mesh=mesh,
        in_specs=(
            P("ctx", "head"),
            P("ctx", "head"),
            P("ctx", "head"),
            P("ctx", "head"),
            P("ctx", "head"),
            P(),
            P("head", None),
        ),
        out_specs=P("ctx", "head"),
        check_vma=False,
    )
```

```python
import jax
import jax.numpy as jnp
from jax import lax
from jax.experimental import pallas as pl
from jax.experimental.pallas import tpu as pltpu
from jax.sharding import PartitionSpec as P

DK = 128
DV = 256
CH = 128
F32 = jnp.float32
BF16 = jnp.bfloat16
MESH = pl.DeviceIdType.MESH

NX = 4
NZ = 8
PIECE = 64
CROSS = 2
REACH = 4


def dot(a, b, dims):
    return lax.dot_general(a, b, (dims, ((), ())), preferred_element_type=F32)


def layer_kernel(
    seg, g_h, k_h, v_h, q_h, gate_h, proj_h, out_h,
    g, k, v, q, cum, state_f, state, starts, weights, decay,
    mixed, reach, gate, wo, wp, hid, hid_peer, send, recv, res, own, ahead_of,
    p1, a1, xs, acc, t_out, a_out, t_in, a_in, plane, p3, e_in,
    s_p1, r_p1, s_a1, r_a1, s_p2, r_p2, s_a2, r_a2, s_p3, r_p3,
    s_w1, r_w1, s_wx, r_wx, s_wf, r_wf, s_ws, r_ws,
    s_hid, r_hid, s_rs, r_rs, s_load, s_out,
):
    ctx = lax.axis_index("ctx")
    y = lax.axis_index("head")
    z = ctx // (2 * NX)
    me = ctx % (2 * NX)
    x = me // 2
    core = me % 2
    base = z * (2 * NX)
    pair = y + 1 - 2 * (y % 2)
    over = 3 - y
    over_pair = over + 1 - 2 * (over % 2)
    xr = (x + 1) % NX
    xl = (x + NX - 1) % NX
    xo = (x + 2) % NX
    tokens = hid.shape[0]
    blocks = tokens // CH
    chunks = tokens // PIECE
    heads = reach.shape[1] // DK
    width = wo.shape[2]
    depth = wo.shape[1]
    slab = depth // (2 * NX)
    part = p1.shape[2]

    def rdma(src, dst, ssem, rsem, c, h):
        return pltpu.make_async_remote_copy(
            src_ref=src, dst_ref=dst, send_sem=ssem, recv_sem=rsem,
            device_id={"ctx": c, "head": h}, device_id_type=MESH,
        )

    def arrived(dst, ssem, rsem):
        rdma(dst, dst, ssem, rsem, ctx, pair).wait_recv()

    def left(src, ssem, rsem):
        rdma(src, src, ssem, rsem, ctx, pair).wait_send()

    mine_cols = pl.ds(pl.multiple_of(y * width, width), width)
    over_cols = pl.ds(pl.multiple_of(over * width, width), width)
    pair_cols = pl.ds(pl.multiple_of(pair * width, width), width)
    loads = [
        pltpu.make_async_copy(src, dst, s_load.at[i])
        for i, (src, dst) in enumerate(
            (
                (g_h, g), (k_h, k), (v_h, v), (q_h, q), (gate_h, gate),
                (proj_h.at[:, over_cols], wo.at[1]), (proj_h.at[:, mine_cols], wo.at[0]),
                (proj_h.at[:, pair_cols], wo.at[2]),
            )
        )
    ]
    for load in loads[:3]:
        load.start()

    barrier = pltpu.get_barrier_semaphore()

    def greet(c, h):
        pl.semaphore_signal(barrier, inc=1, device_id={"ctx": c, "head": h}, device_id_type=MESH)

    greet(ctx, pair)
    greet(ctx, over)
    for step in range(1, 2 * NX):
        greet(base + (me + step) % (2 * NX), y)
    for far in range(1, REACH + 1):

        @pl.when(z + far < NZ)
        def _():
            greet(ctx + far * 2 * NX, y)

        @pl.when(z - far >= 0)
        def _():
            greet(ctx - far * 2 * NX, y)

    ahead = jnp.minimum(NZ - 1 - z, REACH)
    behind = jnp.minimum(z, REACH)
    pl.semaphore_wait(barrier, 2 * NX + 1 + ahead + behind)

    units = (
        (1, 0, slab // 2, pair, 3 - pair),
        (1, slab // 2, slab // 2, pair, 3 - pair),
        (0, 0, slab, pair, pair),
        (3, 0, slab, over, over_pair),
        (2, 0, slab, over, over),
    )

    def unit_rows(u, xx, cc, half=None):
        _, first, size, _, _ = units[u]
        if half is not None:
            size = size // 2
            first = first + half * size
        return pl.ds(pl.multiple_of((xx * 2 + cc) * slab + first, size), size)

    at_r = base + xr * 2 + core
    at_l = base + xl * 2 + core
    sib = base + x * 2 + 1 - core

    def w1(u):
        j, _, _, to, block = units[u]
        rows = unit_rows(u, x, core)
        cols = pl.ds(pl.multiple_of(block * width, width), width)
        return rdma(proj_h.at[rows, cols], wp.at[j, rows], s_w1.at[u], r_w1.at[u], ctx, to)

    def along(u, rows, s, r, item, to):
        j = units[u][0]
        return rdma(wp.at[j, rows], wp.at[j, rows], s.at[u, item], r.at[u, item], to, y)

    def wait_in(u, rows, s, r, item):
        arrived(wp.at[units[u][0], rows], s.at[u, item], r.at[u, item])

    def relays(u, cc):
        return (
            unit_rows(u, x, cc), unit_rows(u, xl, cc), unit_rows(u, xr, cc),
            unit_rows(u, xo, cc, 0), unit_rows(u, xo, cc, 1),
        )

    def stage_a(u):
        here = unit_rows(u, x, core)
        arrived(wp.at[units[u][0], here], s_w1.at[u], r_w1.at[u])
        along(u, here, s_wx, r_wx, 0, at_r).start()
        along(u, here, s_wx, r_wx, 1, at_l).start()
        along(u, here, s_ws, r_ws, 0, sib).start()

    def stage_b(u):
        wait_in(u, unit_rows(u, xl, core), s_wx, r_wx, 0)
        along(u, unit_rows(u, xl, core, 0), s_wf, r_wf, 0, at_r).start()
        along(u, unit_rows(u, xl, core), s_ws, r_ws, 1, sib).start()
        wait_in(u, unit_rows(u, xr, core), s_wx, r_wx, 1)
        along(u, unit_rows(u, xr, core, 1), s_wf, r_wf, 1, at_l).start()
        along(u, unit_rows(u, xr, core), s_ws, r_ws, 2, sib).start()

    def stage_c(u):
        wait_in(u, unit_rows(u, xo, core, 0), s_wf, r_wf, 0)
        along(u, unit_rows(u, xo, core, 0), s_ws, r_ws, 3, sib).start()
        wait_in(u, unit_rows(u, xo, core, 1), s_wf, r_wf, 1)
        along(u, unit_rows(u, xo, core, 1), s_ws, r_ws, 4, sib).start()

    def stage_d(u):
        for item, rows in enumerate(relays(u, 1 - core)):
            wait_in(u, rows, s_ws, r_ws, item)

    def weights_left(u):
        j = units[u][0]
        here = unit_rows(u, x, core)
        left(wp.at[j, here], s_w1.at[u], r_w1.at[u])
        for item in range(2):
            left(wp.at[j, here], s_wx.at[u, item], r_wx.at[u, item])
            left(wp.at[j, unit_rows(u, x, core, 0)], s_wf.at[u, item], r_wf.at[u, item])
        for item, rows in enumerate(relays(u, core)):
            left(wp.at[j, rows], s_ws.at[u, item], r_ws.at[u, item])

    for u in (0, 1, 3, 4):
        w1(u).start()

    block_rows = lax.broadcasted_iota(jnp.int32, (CH, CH), 0)
    block_cols = lax.broadcasted_iota(jnp.int32, (CH, CH), 1)
    causal = block_cols <= block_rows
    ones = causal.astype(F32).astype(BF16)
    state_f[...] = jnp.zeros_like(state_f)
    decay[...] = jnp.ones_like(decay)
    wide = p1.shape[3]
    halves = p1.shape[0]
    group = heads // halves

    def rows_at(c, size):
        return pl.ds(pl.multiple_of(c * size, size), size)

    def head_keys(h):
        return slice(h * DK, (h + 1) * DK)

    def head_vals(h):
        return slice(h * DV, (h + 1) * DV)

    for load in loads[:3]:
        load.wait()
    for load in loads[3:]:
        load.start()

    def state_step(f, b):
        lanes = slice(f * wide, (f + 1) * wide)
        rows = rows_at(b, CH)
        at = ctx * blocks + b
        same = jnp.logical_and(seg[at] == seg[jnp.maximum(at - 1, 0)], at > 0)
        keep = jnp.where(same, 1.0, 0.0)
        sums = dot(ones, g[rows, lanes], ((1,), (0,)))
        cum[rows, lanes] = sums
        last = sums[CH - 1 : CH, :]
        kept = (k[rows, lanes].astype(F32) * jnp.exp(last - sums)).astype(BF16)
        fall = jnp.exp(last)
        weight = decay[f] * keep
        weights[b, :, lanes] = weight
        decay[f] = weight * fall
        for i in range(group):
            kc = head_keys(i)
            start = state_f[f, :, kc] * keep
            starts[b, :, head_keys(f * group + i)] = start.astype(BF16)
            added = dot(v[rows, head_vals(f * group + i)], kept[:, kc], ((0,), (0,)))
            state_f[f, :, kc] = start * fall[:, kc] + added

    def rows_of(i):
        return pl.ds(pl.multiple_of(i * part, part), part)

    for f in range(halves):

        def step_of(b, carry):
            state_step(f, b)
            return carry

        lax.fori_loop(0, blocks, step_of, 0, unroll=8)
        state[f] = state_f[f].astype(BF16)
        for step in range(1, 2 * NX):
            i = (me + step) % (2 * NX)
            rdma(decay.at[f], a1.at[f, me], s_a1.at[f, i], r_a1.at[f, me], base + i, y).start()
            rdma(
                state.at[f, rows_of(i), :], p1.at[f, me], s_p1.at[f, i], r_p1.at[f, me], base + i, y
            ).start()
        p1[f, me] = state[f, rows_of(me), :]
        a1[f, me] = decay[f]

    def block_step(b, carry):
        rows = rows_at(b, CH)
        sums = cum[rows, :]
        dq = q[rows, :].astype(F32) * jnp.exp(sums) * DK ** (-0.5)
        dk = (k[rows, :].astype(F32) * jnp.exp(-sums)).astype(BF16)
        reach[rows, :] = (dq * weights[b]).astype(BF16)
        dq = dq.astype(BF16)
        for h in range(heads):
            kc = head_keys(h)
            vc = head_vals(h)
            scores = dot(dq[:, kc], dk[:, kc], ((1,), (1,)))
            probs = jnp.where(causal, scores, 0.0).astype(BF16)
            out = dot(probs, v[rows, vc], ((1,), (0,)))
            out += dot(dq[:, kc], starts[b, :, kc], ((1,), (1,)))
            mixed[rows, vc] = out.astype(BF16)
        return carry

    loads[3].wait()
    first_part = 3
    lax.fori_loop(0, first_part, block_step, 0, unroll=first_part)


    for f in range(halves):
        for step in range(1, 2 * NX):
            i = (me + step) % (2 * NX)
            arrived(a1.at[f, i], s_a1.at[f, i], r_a1.at[f, i])
            arrived(p1.at[f, i], s_p1.at[f, i], r_p1.at[f, i])
        run = jnp.zeros((part, wide), F32)
        scale = jnp.ones((1, wide), F32)
        for i in range(2 * NX):
            xs[f, i] = run
            acc[f, i] = scale
            run = run * a1[f, i] + p1[f, i].astype(F32)
            scale = scale * a1[f, i]
        t_out[f] = run.astype(BF16)
        a_out[f] = scale
        for far in range(1, REACH + 1):

            @pl.when(z + far < NZ)
            def _():
                to = ctx + far * 2 * NX
                n = far - 1
                rdma(a_out.at[f], a_in.at[f, n], s_a2.at[f, n], r_a2.at[f, n], to, y).start()
                rdma(t_out.at[f], t_in.at[f, n], s_p2.at[f, n], r_p2.at[f, n], to, y).start()

        stage_a(f)

    w1(2).start()
    lax.fori_loop(first_part, blocks, block_step, 0, unroll=blocks - first_part)

    for f in range(halves):
        plane[...] = jnp.zeros_like(plane)
        for far in range(REACH, 0, -1):

            @pl.when(z - far >= 0)
            def _():
                n = far - 1
                arrived(a_in.at[f, n], s_a2.at[f, n], r_a2.at[f, n])
                arrived(t_in.at[f, n], s_p2.at[f, n], r_p2.at[f, n])
                plane[...] = plane[...] * a_in[f, n] + t_in[f, n].astype(F32)

        for i in range(2 * NX):
            p3[f, i] = (xs[f, i] + acc[f, i] * plane[...]).astype(BF16)
        for step in range(1, 2 * NX):
            i = (me + step) % (2 * NX)
            rdma(
                p3.at[f, i], e_in.at[f, rows_of(me), :], s_p3.at[f, i], r_p3.at[f, me], base + i, y
            ).start()
        e_in[f, rows_of(me), :] = p3[f, me]

    stage_b(0)
    stage_b(1)
    loads[4].wait()

    for f in range(halves):
        for step in range(1, 2 * NX):
            i = (me + step) % (2 * NX)
            arrived(e_in.at[f, rows_of(i), :], s_p3.at[f, i], r_p3.at[f, i])

    straight = chunks - CROSS

    def hidden_step(step, carry):
        c = jnp.where(step < 2 * CROSS, step // 2 + (step % 2) * straight, step - CROSS)
        to = jnp.where(c < straight, pair, over)
        rows = rows_at(c, PIECE)
        for h in range(heads):
            kc = head_keys(h)
            vc = head_vals(h)
            full = mixed[rows, vc].astype(F32)
            full += dot(reach[rows, kc], e_in[h // group, :, head_keys(h % group)], ((1,), (1,)))
            mean = jnp.mean(full * full, axis=-1, keepdims=True)
            val = gate[rows, vc].astype(F32)
            silu = val / (1.0 + jnp.exp(-val))
            hid[rows, vc] = (full * lax.rsqrt(mean + 1e-5) * silu).astype(BF16)
        rdma(hid.at[rows, :], hid_peer.at[rows, :], s_hid.at[c], r_hid.at[c], ctx, to).start()
        return carry

    lax.fori_loop(0, 2 * CROSS, hidden_step, 0)
    stage_c(0)
    lax.fori_loop(2 * CROSS, chunks, hidden_step, 0)

    stage_c(1)
    stage_a(2)
    for load in loads[5:]:
        load.wait()
    stage_d(0)
    stage_d(1)

    tile = 512

    def columns(do):
        def column(n, carry):
            do(pl.ds(pl.multiple_of(n * tile, tile), tile))
            return carry

        lax.fori_loop(0, width // tile, column, 0)

    def own_sums(first, count, j):
        rows = pl.ds(first * PIECE, count * PIECE)

        def both_parts(cols):
            total = dot(hid[rows, :], wo[0, :, cols], ((1,), (0,)))
            own[rows, cols] = total + dot(hid_peer[rows, :], wp[j, :, cols], ((1,), (0,)))

        columns(both_parts)

    def piece_at(step):
        late = step - (chunks - 2 * CROSS + 1)
        crossed = jnp.logical_and(late >= 0, late % 2 == 0)
        behind_cross = step - (late + 1) // 2
        return jnp.where(late < 0, step, jnp.where(crossed, straight + late // 2, behind_cross))

    def main_step(step, carry):
        c = piece_at(step)
        crossed = c >= straight
        to = jnp.where(crossed, pair, over)
        jo = jnp.where(crossed, 2, 1)
        jp = jnp.where(crossed, 3, 1)
        rows = rows_at(c, PIECE)

        def own_part(cols):
            ahead_of[:, cols] = dot(hid[rows, :], wo[jo, :, cols], ((1,), (0,)))

        def pair_part(cols):
            total = ahead_of[:, cols] + dot(hid_peer[rows, :], wp[jp, :, cols], ((1,), (0,)))
            send[rows, cols] = total.astype(BF16)

        columns(own_part)
        arrived(hid_peer.at[rows, :], s_hid.at[c], r_hid.at[c])
        columns(pair_part)
        rdma(send.at[rows, :], recv.at[rows, :], s_rs.at[c], r_rs.at[c], ctx, to).start()

        def at(when, *actions):
            @pl.when(step == when)
            def _():
                for action, *args in actions:
                    action(*args)

        at(3, (stage_b, 2), (stage_a, 3))
        at(5, (stage_c, 2))
        at(6, (stage_b, 3), (stage_a, 4))
        at(7, (stage_d, 2), (own_sums, 0, 4, 0))
        at(8, (stage_c, 3))
        at(9, (stage_b, 4), (own_sums, 4, 4, 0))
        at(10, (stage_d, 3))
        at(11, (stage_c, 4), (own_sums, 8, 4, 0))
        return carry

    lax.fori_loop(0, chunks, main_step, 0)
    stage_d(4)
    own_sums(12, straight - 12, 0)
    own_sums(straight, CROSS, 2)

    for f in range(halves):
        for step in range(1, 2 * NX):
            i = (me + step) % (2 * NX)
            left(decay.at[f], s_a1.at[f, i], r_a1.at[f, i])
            left(p1.at[f, i], s_p1.at[f, i], r_p1.at[f, i])
            left(p3.at[f, i], s_p3.at[f, i], r_p3.at[f, i])
        for far in range(1, REACH + 1):

            @pl.when(z + far < NZ)
            def _():
                n = far - 1
                left(a_out.at[f], s_a2.at[f, n], r_a2.at[f, n])
                left(t_out.at[f], s_p2.at[f, n], r_p2.at[f, n])

    for u in range(len(units)):
        weights_left(u)

    def hidden_left(c, carry):
        rows = rows_at(c, PIECE)
        left(hid.at[rows, :], s_hid.at[c], r_hid.at[c])
        return carry

    lax.fori_loop(0, chunks, hidden_left, 0)

    def store(c):
        rows = rows_at(c, PIECE)
        return pltpu.make_async_copy(res.at[rows, :], out_h.at[rows, :], s_out.at[c])

    def result_step(step, carry):
        c = piece_at(step)
        rows = rows_at(c, PIECE)
        arrived(recv.at[rows, :], s_rs.at[c], r_rs.at[c])
        res[rows, :] = (own[rows, :] + recv[rows, :].astype(F32)).astype(BF16)
        store(c).start()

        @pl.when(step >= 2)
        def _():
            before = piece_at(step - 2)
            store(before).wait()
            left(send.at[rows_at(before, PIECE), :], s_rs.at[before], r_rs.at[before])

        return carry

    lax.fori_loop(0, chunks, result_step, 0)
    for step in range(chunks - 2, chunks):
        store(piece_at(step)).wait()
        left(send.at[rows_at(piece_at(step), PIECE), :], s_rs.at[piece_at(step)], r_rs.at[piece_at(step)])


def copy_kernel(src, dst, held, s_in, s_out):
    parts = s_in.shape[0]
    size = src.shape[0] // parts
    reads = [
        pltpu.make_async_copy(src.at[pl.ds(i * size, size)], held.at[pl.ds(i * size, size)], s_in.at[i])
        for i in range(parts)
    ]
    writes = [
        pltpu.make_async_copy(held.at[pl.ds(i * size, size)], dst.at[pl.ds(i * size, size)], s_out.at[i])
        for i in range(parts)
    ]
    for read in reads:
        read.start()
    for read, write in zip(reads, writes, strict=True):
        read.wait()
        write.start()
    for write in writes:
        write.wait()


def shards(queries, keys, values, log_gate, out_gate, segment_ids, final_projector):
    tokens = queries.shape[0]
    keys_wide = queries.shape[1]
    vals_wide = values.shape[1]
    depth, full = final_projector.shape
    width = full // 4
    slots = 2 * NX
    part = DV // slots
    blocks = tokens // CH
    chunks = tokens // PIECE
    halves = 2
    wide = keys_wide // halves

    vm = pltpu.VMEM
    dma = pltpu.SemaphoreType.DMA
    projected = pl.pallas_call(
        layer_kernel,
        in_specs=[pl.BlockSpec(memory_space=pltpu.SMEM)] + [pl.BlockSpec(memory_space=pl.ANY)] * 6,
        out_specs=pl.BlockSpec(memory_space=pl.ANY),
        out_shape=jax.ShapeDtypeStruct((tokens, width), BF16),
        scratch_shapes=[
            vm((tokens, keys_wide), BF16),
            vm((tokens, keys_wide), BF16),
            vm((tokens, vals_wide), BF16),
            vm((tokens, keys_wide), BF16),
            vm((tokens, keys_wide), F32),
            vm((halves, DV, wide), F32),
            vm((halves, DV, wide), BF16),
            vm((blocks, DV, keys_wide), BF16),
            vm((blocks, 1, keys_wide), F32),
            vm((halves, 1, wide), F32),
            vm((tokens, vals_wide), BF16),
            vm((tokens, keys_wide), BF16),
            vm((tokens, vals_wide), BF16),
            vm((3, depth, width), BF16),
            vm((4, depth, width), BF16),
            vm((tokens, vals_wide), BF16),
            vm((tokens, vals_wide), BF16),
            vm((tokens, width), BF16),
            vm((tokens, width), BF16),
            vm((tokens, width), BF16),
            vm((tokens, width), F32),
            vm((PIECE, width), F32),
            vm((halves, slots, part, wide), BF16),
            vm((halves, slots, 1, wide), F32),
            vm((halves, slots, part, wide), F32),
            vm((halves, slots, 1, wide), F32),
            vm((halves, part, wide), BF16),
            vm((halves, 1, wide), F32),
            vm((halves, REACH, part, wide), BF16),
            vm((halves, REACH, 1, wide), F32),
            vm((part, wide), F32),
            vm((halves, slots, part, wide), BF16),
            vm((halves, DV, wide), BF16),
            dma((halves, slots)), dma((halves, slots)),
            dma((halves, slots)), dma((halves, slots)),
            dma((halves, REACH)), dma((halves, REACH)),
            dma((halves, REACH)), dma((halves, REACH)),
            dma((halves, slots)), dma((halves, slots)),
            dma((5,)), dma((5,)),
            dma((5, 2)), dma((5, 2)),
            dma((5, 2)), dma((5, 2)),
            dma((5, 5)), dma((5, 5)),
            dma((chunks,)), dma((chunks,)),
            dma((chunks,)), dma((chunks,)),
            dma((8,)),
            dma((chunks,)),
        ],
        compiler_params=pltpu.CompilerParams(
            collective_id=0, has_side_effects=True, vmem_limit_bytes=58 * 2**20
        ),
    )(segment_ids, log_gate, keys, values, queries, out_gate, final_projector)
    return pl.pallas_call(
        copy_kernel,
        in_specs=[pl.BlockSpec(memory_space=pl.ANY)],
        out_specs=pl.BlockSpec(memory_space=pl.ANY),
        out_shape=jax.ShapeDtypeStruct((tokens, width), BF16),
        scratch_shapes=[vm((tokens, width), BF16), dma((4,)), dma((4,))],
        compiler_params=pltpu.CompilerParams(vmem_limit_bytes=60 * 2**20),
    )(projected)


def solution(mesh):
    return jax.shard_map(
        shards,
        mesh=mesh,
        in_specs=(
            P("ctx", "head"),
            P("ctx", "head"),
            P("ctx", "head"),
            P("ctx", "head"),
            P("ctx", "head"),
            P(),
            P("head", None),
        ),
        out_specs=P("ctx", "head"),
        check_vma=False,
    )
```

```python
import jax
import jax.numpy as jnp
from jax import lax
from jax.experimental import pallas as pl
from jax.experimental.pallas import tpu as pltpu
from jax.sharding import PartitionSpec as P

DK = 128
DV = 256
CH = 128
F32 = jnp.float32
BF16 = jnp.bfloat16
MESH = pl.DeviceIdType.MESH

NX = 4
NZ = 8
PIECE = 64
CROSS = 2
REACH = 4


def dot(a, b, dims):
    return lax.dot_general(a, b, (dims, ((), ())), preferred_element_type=F32)


def layer_kernel(
    seg, g_h, k_h, v_h, q_h, gate_h, proj_h, out,
    g, k, v, q, cum, state_f, state, starts, weights, decay, weight_now,
    mixed, reach, gate, wo, wp, hid, hid_peer, send, recv, own, ahead_of,
    p1, a1, xs, acc, t_out, a_out, t_in, a_in, plane, p3, e_in,
    s_p1, r_p1, s_a1, r_a1, s_p2, r_p2, s_a2, r_a2, s_p3, r_p3,
    s_w1, r_w1, s_wx, r_wx, s_wf, r_wf, s_ws, r_ws,
    s_hid, r_hid, s_rs, r_rs, s_load,
):
    ctx = lax.axis_index("ctx")
    y = lax.axis_index("head")
    z = ctx // (2 * NX)
    me = ctx % (2 * NX)
    x = me // 2
    core = me % 2
    base = z * (2 * NX)
    pair = y + 1 - 2 * (y % 2)
    over = 3 - y
    over_pair = over + 1 - 2 * (over % 2)
    xr = (x + 1) % NX
    xl = (x + NX - 1) % NX
    xo = (x + 2) % NX
    tokens = hid.shape[0]
    blocks = tokens // CH
    chunks = tokens // PIECE
    heads = reach.shape[1] // DK
    width = wo.shape[2]
    depth = wo.shape[1]
    slab = depth // (2 * NX)
    part = p1.shape[2]

    def rdma(src, dst, ssem, rsem, c, h):
        return pltpu.make_async_remote_copy(
            src_ref=src, dst_ref=dst, send_sem=ssem, recv_sem=rsem,
            device_id={"ctx": c, "head": h}, device_id_type=MESH,
        )

    def arrived(dst, ssem, rsem):
        rdma(dst, dst, ssem, rsem, ctx, pair).wait_recv()

    def left(src, ssem, rsem):
        rdma(src, src, ssem, rsem, ctx, pair).wait_send()

    mine_cols = pl.ds(pl.multiple_of(y * width, width), width)
    over_cols = pl.ds(pl.multiple_of(over * width, width), width)
    pair_cols = pl.ds(pl.multiple_of(pair * width, width), width)
    loads = [
        pltpu.make_async_copy(src, dst, s_load.at[i])
        for i, (src, dst) in enumerate(
            (
                (g_h, g), (k_h, k), (v_h, v), (q_h, q), (gate_h, gate),
                (proj_h.at[:, over_cols], wo.at[1]), (proj_h.at[:, mine_cols], wo.at[0]),
                (proj_h.at[:, pair_cols], wo.at[2]),
            )
        )
    ]
    for load in loads[:3]:
        load.start()

    barrier = pltpu.get_barrier_semaphore()

    def greet(c, h):
        pl.semaphore_signal(barrier, inc=1, device_id={"ctx": c, "head": h}, device_id_type=MESH)

    greet(ctx, pair)
    greet(ctx, over)
    for step in range(1, 2 * NX):
        greet(base + (me + step) % (2 * NX), y)
    for far in range(1, REACH + 1):

        @pl.when(z + far < NZ)
        def _():
            greet(ctx + far * 2 * NX, y)

        @pl.when(z - far >= 0)
        def _():
            greet(ctx - far * 2 * NX, y)

    ahead = jnp.minimum(NZ - 1 - z, REACH)
    behind = jnp.minimum(z, REACH)
    pl.semaphore_wait(barrier, 2 * NX + 1 + ahead + behind)

    units = (
        (1, 0, slab // 2, pair, 3 - pair),
        (1, slab // 2, slab // 2, pair, 3 - pair),
        (0, 0, slab, pair, pair),
        (3, 0, slab, over, over_pair),
        (2, 0, slab, over, over),
    )

    def unit_rows(u, xx, cc, half=None):
        _, first, size, _, _ = units[u]
        if half is not None:
            size = size // 2
            first = first + half * size
        return pl.ds(pl.multiple_of((xx * 2 + cc) * slab + first, size), size)

    at_r = base + xr * 2 + core
    at_l = base + xl * 2 + core
    sib = base + x * 2 + 1 - core

    def w1(u):
        j, _, _, to, block = units[u]
        rows = unit_rows(u, x, core)
        cols = pl.ds(pl.multiple_of(block * width, width), width)
        return rdma(proj_h.at[rows, cols], wp.at[j, rows], s_w1.at[u], r_w1.at[u], ctx, to)

    def along(u, rows, s, r, item, to):
        j = units[u][0]
        return rdma(wp.at[j, rows], wp.at[j, rows], s.at[u, item], r.at[u, item], to, y)

    def wait_in(u, rows, s, r, item):
        arrived(wp.at[units[u][0], rows], s.at[u, item], r.at[u, item])

    def relays(u, cc):
        return (
            unit_rows(u, x, cc), unit_rows(u, xl, cc), unit_rows(u, xr, cc),
            unit_rows(u, xo, cc, 0), unit_rows(u, xo, cc, 1),
        )

    def stage_a(u):
        here = unit_rows(u, x, core)
        arrived(wp.at[units[u][0], here], s_w1.at[u], r_w1.at[u])
        along(u, here, s_wx, r_wx, 0, at_r).start()
        along(u, here, s_wx, r_wx, 1, at_l).start()
        along(u, here, s_ws, r_ws, 0, sib).start()

    def stage_b(u):
        wait_in(u, unit_rows(u, xl, core), s_wx, r_wx, 0)
        along(u, unit_rows(u, xl, core, 0), s_wf, r_wf, 0, at_r).start()
        along(u, unit_rows(u, xl, core), s_ws, r_ws, 1, sib).start()
        wait_in(u, unit_rows(u, xr, core), s_wx, r_wx, 1)
        along(u, unit_rows(u, xr, core, 1), s_wf, r_wf, 1, at_l).start()
        along(u, unit_rows(u, xr, core), s_ws, r_ws, 2, sib).start()

    def stage_c(u):
        wait_in(u, unit_rows(u, xo, core, 0), s_wf, r_wf, 0)
        along(u, unit_rows(u, xo, core, 0), s_ws, r_ws, 3, sib).start()
        wait_in(u, unit_rows(u, xo, core, 1), s_wf, r_wf, 1)
        along(u, unit_rows(u, xo, core, 1), s_ws, r_ws, 4, sib).start()

    def stage_d(u):
        for item, rows in enumerate(relays(u, 1 - core)):
            wait_in(u, rows, s_ws, r_ws, item)

    def weights_left(u):
        j = units[u][0]
        here = unit_rows(u, x, core)
        left(wp.at[j, here], s_w1.at[u], r_w1.at[u])
        for item in range(2):
            left(wp.at[j, here], s_wx.at[u, item], r_wx.at[u, item])
            left(wp.at[j, unit_rows(u, x, core, 0)], s_wf.at[u, item], r_wf.at[u, item])
        for item, rows in enumerate(relays(u, core)):
            left(wp.at[j, rows], s_ws.at[u, item], r_ws.at[u, item])

    for u in (0, 1, 3, 4):
        w1(u).start()

    block_rows = lax.broadcasted_iota(jnp.int32, (CH, CH), 0)
    block_cols = lax.broadcasted_iota(jnp.int32, (CH, CH), 1)
    causal = block_cols <= block_rows
    ones = causal.astype(F32).astype(BF16)
    state_f[...] = jnp.zeros_like(state_f)
    weight_now[...] = jnp.ones_like(weight_now)
    wide = p1.shape[3]
    halves = p1.shape[0]
    group = heads // halves

    def rows_at(c, size):
        return pl.ds(pl.multiple_of(c * size, size), size)

    def head_keys(h):
        return slice(h * DK, (h + 1) * DK)

    def head_vals(h):
        return slice(h * DV, (h + 1) * DV)

    for load in loads[:3]:
        load.wait()
    for load in loads[3:]:
        load.start()

    def same_stream(b):
        at = ctx * blocks + b
        same = jnp.logical_and(seg[at] == seg[jnp.maximum(at - 1, 0)], at > 0)
        return jnp.where(same, 1.0, 0.0)

    def state_step(f, b):
        lanes = slice(f * wide, (f + 1) * wide)
        rows = rows_at(b, CH)
        keep = same_stream(b)
        sums = dot(ones, g[rows, lanes], ((1,), (0,)))
        cum[rows, lanes] = sums
        last = sums[CH - 1 : CH, :]
        kept = (k[rows, lanes].astype(F32) * jnp.exp(last - sums)).astype(BF16)
        fall = jnp.exp(last)
        weight = weight_now[f] * keep
        weights[b, :, lanes] = weight
        weight_now[f] = weight * fall
        for i in range(group):
            kc = head_keys(i)
            start = state_f[f, :, kc] * keep
            starts[b, :, head_keys(f * group + i)] = start.astype(BF16)
            added = dot(v[rows, head_vals(f * group + i)], kept[:, kc], ((0,), (0,)))
            state_f[f, :, kc] = start * fall[:, kc] + added

    def rows_of(i):
        return pl.ds(pl.multiple_of(i * part, part), part)

    flags = [same_stream(b) for b in range(blocks)]
    through = flags[0]
    for flag in flags[1:]:
        through = through * flag
    total = dot(jnp.ones((16, tokens), BF16), g[...], ((1,), (0,)))[:1]
    decay[...] = jnp.exp(total) * through
    for step in range(1, 2 * NX):
        i = (me + step) % (2 * NX)
        rdma(decay, a1.at[me], s_a1.at[i], r_a1.at[me], base + i, y).start()
    a1[me] = decay[...]

    for f in range(halves):

        def step_of(b, carry):
            state_step(f, b)
            return carry

        lax.fori_loop(0, blocks, step_of, 0, unroll=8)
        state[f] = state_f[f].astype(BF16)
        for step in range(1, 2 * NX):
            i = (me + step) % (2 * NX)
            rdma(
                state.at[f, rows_of(i), :], p1.at[f, me], s_p1.at[f, i], r_p1.at[f, me], base + i, y
            ).start()
        p1[f, me] = state[f, rows_of(me), :]

    def block_step(b, carry):
        rows = rows_at(b, CH)
        sums = cum[rows, :]
        dq = q[rows, :].astype(F32) * jnp.exp(sums) * DK ** (-0.5)
        dk = (k[rows, :].astype(F32) * jnp.exp(-sums)).astype(BF16)
        reach[rows, :] = (dq * weights[b]).astype(BF16)
        dq = dq.astype(BF16)
        for h in range(heads):
            kc = head_keys(h)
            vc = head_vals(h)
            scores = dot(dq[:, kc], dk[:, kc], ((1,), (1,)))
            probs = jnp.where(causal, scores, 0.0).astype(BF16)
            out = dot(probs, v[rows, vc], ((1,), (0,)))
            out += dot(dq[:, kc], starts[b, :, kc], ((1,), (1,)))
            mixed[rows, vc] = out.astype(BF16)
        return carry

    loads[3].wait()
    first_part = 3
    lax.fori_loop(0, first_part, block_step, 0, unroll=first_part)


    for step in range(1, 2 * NX):
        i = (me + step) % (2 * NX)
        arrived(a1.at[i], s_a1.at[i], r_a1.at[i])
    scale = jnp.ones_like(decay[...])
    for i in range(2 * NX):
        acc[i] = scale
        scale = scale * a1[i]
    a_out[...] = scale
    for far in range(1, REACH + 1):

        @pl.when(z + far < NZ)
        def _():
            n = far - 1
            rdma(a_out, a_in.at[n], s_a2.at[n], r_a2.at[n], ctx + far * 2 * NX, y).start()

    for f in range(halves):
        for step in range(1, 2 * NX):
            i = (me + step) % (2 * NX)
            arrived(p1.at[f, i], s_p1.at[f, i], r_p1.at[f, i])
        run = jnp.zeros((part, wide), F32)
        lanes = slice(f * wide, (f + 1) * wide)
        for i in range(2 * NX):
            xs[f, i] = run
            run = run * a1[i, :, lanes] + p1[f, i].astype(F32)
        t_out[f] = run.astype(BF16)
        for far in range(1, REACH + 1):

            @pl.when(z + far < NZ)
            def _():
                to = ctx + far * 2 * NX
                n = far - 1
                rdma(t_out.at[f], t_in.at[f, n], s_p2.at[f, n], r_p2.at[f, n], to, y).start()

        stage_a(f)

    w1(2).start()
    lax.fori_loop(first_part, blocks, block_step, 0, unroll=blocks - first_part)

    for f in range(halves):
        lanes = slice(f * wide, (f + 1) * wide)
        plane[...] = jnp.zeros_like(plane)
        for far in range(REACH, 0, -1):

            @pl.when(z - far >= 0)
            def _():
                n = far - 1
                if f == 0:
                    arrived(a_in.at[n], s_a2.at[n], r_a2.at[n])
                arrived(t_in.at[f, n], s_p2.at[f, n], r_p2.at[f, n])
                plane[...] = plane[...] * a_in[n, :, lanes] + t_in[f, n].astype(F32)

        for i in range(2 * NX):
            p3[f, i] = (xs[f, i] + acc[i, :, lanes] * plane[...]).astype(BF16)
        for step in range(1, 2 * NX):
            i = (me + step) % (2 * NX)
            rdma(
                p3.at[f, i], e_in.at[f, rows_of(me), :], s_p3.at[f, i], r_p3.at[f, me], base + i, y
            ).start()
        e_in[f, rows_of(me), :] = p3[f, me]

    stage_b(0)
    stage_b(1)
    loads[4].wait()

    for f in range(halves):
        for step in range(1, 2 * NX):
            i = (me + step) % (2 * NX)
            arrived(e_in.at[f, rows_of(i), :], s_p3.at[f, i], r_p3.at[f, i])

    straight = chunks - CROSS

    def hidden_step(step, carry):
        c = jnp.where(step < 2 * CROSS, step // 2 + (step % 2) * straight, step - CROSS)
        to = jnp.where(c < straight, pair, over)
        rows = rows_at(c, PIECE)
        for h in range(heads):
            kc = head_keys(h)
            vc = head_vals(h)
            full = mixed[rows, vc].astype(F32)
            full += dot(reach[rows, kc], e_in[h // group, :, head_keys(h % group)], ((1,), (1,)))
            mean = jnp.mean(full * full, axis=-1, keepdims=True)
            val = gate[rows, vc].astype(F32)
            silu = val / (1.0 + jnp.exp(-val))
            hid[rows, vc] = (full * lax.rsqrt(mean + 1e-5) * silu).astype(BF16)
        rdma(hid.at[rows, :], hid_peer.at[rows, :], s_hid.at[c], r_hid.at[c], ctx, to).start()
        return carry

    lax.fori_loop(0, 2 * CROSS, hidden_step, 0)
    stage_c(0)
    lax.fori_loop(2 * CROSS, chunks, hidden_step, 0)

    stage_c(1)
    stage_a(2)
    for load in loads[5:]:
        load.wait()
    stage_d(0)
    stage_d(1)

    tile = 512

    def columns(do):
        def column(n, carry):
            do(pl.ds(pl.multiple_of(n * tile, tile), tile))
            return carry

        lax.fori_loop(0, width // tile, column, 0)

    def own_sums(first, count, j):
        rows = pl.ds(first * PIECE, count * PIECE)

        def both_parts(cols):
            total = dot(hid[rows, :], wo[0, :, cols], ((1,), (0,)))
            own[rows, cols] = total + dot(hid_peer[rows, :], wp[j, :, cols], ((1,), (0,)))

        columns(both_parts)

    def piece_at(step):
        late = step - (chunks - 2 * CROSS + 1)
        crossed = jnp.logical_and(late >= 0, late % 2 == 0)
        behind_cross = step - (late + 1) // 2
        return jnp.where(late < 0, step, jnp.where(crossed, straight + late // 2, behind_cross))

    def main_step(step, carry):
        c = piece_at(step)
        crossed = c >= straight
        to = jnp.where(crossed, pair, over)
        jo = jnp.where(crossed, 2, 1)
        jp = jnp.where(crossed, 3, 1)
        rows = rows_at(c, PIECE)

        def own_part(cols):
            ahead_of[:, cols] = dot(hid[rows, :], wo[jo, :, cols], ((1,), (0,)))

        def pair_part(cols):
            total = ahead_of[:, cols] + dot(hid_peer[rows, :], wp[jp, :, cols], ((1,), (0,)))
            send[rows, cols] = total.astype(BF16)

        columns(own_part)
        arrived(hid_peer.at[rows, :], s_hid.at[c], r_hid.at[c])
        columns(pair_part)
        rdma(send.at[rows, :], recv.at[rows, :], s_rs.at[c], r_rs.at[c], ctx, to).start()

        def at(when, *actions):
            @pl.when(step == when)
            def _():
                for action, *args in actions:
                    action(*args)

        at(3, (stage_b, 2), (stage_a, 3))
        at(5, (stage_c, 2))
        at(6, (stage_b, 3), (stage_a, 4))
        at(7, (stage_d, 2), (own_sums, 0, 4, 0))
        at(8, (stage_c, 3))
        at(9, (own_sums, 4, 4, 0))
        at(10, (stage_d, 3))
        at(11, (stage_b, 4), (own_sums, 8, 4, 0))
        at(14, (stage_c, 4))
        return carry

    lax.fori_loop(0, chunks, main_step, 0)
    stage_d(4)
    own_sums(12, straight - 12, 0)
    own_sums(straight, CROSS, 2)

    for f in range(halves):
        for step in range(1, 2 * NX):
            i = (me + step) % (2 * NX)
            if f == 0:
                left(decay, s_a1.at[i], r_a1.at[i])
            left(p1.at[f, i], s_p1.at[f, i], r_p1.at[f, i])
            left(p3.at[f, i], s_p3.at[f, i], r_p3.at[f, i])
        for far in range(1, REACH + 1):

            @pl.when(z + far < NZ)
            def _():
                n = far - 1
                if f == 0:
                    left(a_out, s_a2.at[n], r_a2.at[n])
                left(t_out.at[f], s_p2.at[f, n], r_p2.at[f, n])

    for u in range(len(units)):
        weights_left(u)

    def hidden_left(c, carry):
        rows = rows_at(c, PIECE)
        left(hid.at[rows, :], s_hid.at[c], r_hid.at[c])
        return carry

    lax.fori_loop(0, chunks, hidden_left, 0)

    def result_step(step, carry):
        c = piece_at(step)
        rows = rows_at(c, PIECE)
        arrived(recv.at[rows, :], s_rs.at[c], r_rs.at[c])
        out[rows, :] = (own[rows, :] + recv[rows, :].astype(F32)).astype(BF16)

        @pl.when(step >= 2)
        def _():
            before = piece_at(step - 2)
            left(send.at[rows_at(before, PIECE), :], s_rs.at[before], r_rs.at[before])

        return carry

    lax.fori_loop(0, chunks, result_step, 0)
    for step in range(chunks - 2, chunks):
        left(send.at[rows_at(piece_at(step), PIECE), :], s_rs.at[piece_at(step)], r_rs.at[piece_at(step)])


def copy_kernel(src, dst, sems):
    parts = sems.shape[0]
    size = src.shape[0] // parts
    writes = [
        pltpu.make_async_copy(src.at[pl.ds(i * size, size)], dst.at[pl.ds(i * size, size)], sems.at[i])
        for i in range(parts)
    ]
    for write in writes:
        write.start()
    for write in writes:
        write.wait()


def shards(queries, keys, values, log_gate, out_gate, segment_ids, final_projector):
    tokens = queries.shape[0]
    keys_wide = queries.shape[1]
    vals_wide = values.shape[1]
    depth, full = final_projector.shape
    width = full // 4
    slots = 2 * NX
    part = DV // slots
    blocks = tokens // CH
    chunks = tokens // PIECE
    halves = 2
    wide = keys_wide // halves

    vm = pltpu.VMEM
    dma = pltpu.SemaphoreType.DMA
    projected = pl.pallas_call(
        layer_kernel,
        in_specs=[pl.BlockSpec(memory_space=pltpu.SMEM)] + [pl.BlockSpec(memory_space=pl.ANY)] * 6,
        out_specs=pl.BlockSpec(memory_space=pltpu.VMEM),
        out_shape=pltpu.VMEM((tokens, width), BF16),
        scratch_shapes=[
            vm((tokens, keys_wide), BF16),
            vm((tokens, keys_wide), BF16),
            vm((tokens, vals_wide), BF16),
            vm((tokens, keys_wide), BF16),
            vm((tokens, keys_wide), F32),
            vm((halves, DV, wide), F32),
            vm((halves, DV, wide), BF16),
            vm((blocks, DV, keys_wide), BF16),
            vm((blocks, 1, keys_wide), F32),
            vm((1, keys_wide), F32),
            vm((halves, 1, wide), F32),
            vm((tokens, vals_wide), BF16),
            vm((tokens, keys_wide), BF16),
            vm((tokens, vals_wide), BF16),
            vm((3, depth, width), BF16),
            vm((4, depth, width), BF16),
            vm((tokens, vals_wide), BF16),
            vm((tokens, vals_wide), BF16),
            vm((tokens, width), BF16),
            vm((tokens, width), BF16),
            vm((tokens, width), F32),
            vm((PIECE, width), F32),
            vm((halves, slots, part, wide), BF16),
            vm((slots, 1, keys_wide), F32),
            vm((halves, slots, part, wide), F32),
            vm((slots, 1, keys_wide), F32),
            vm((halves, part, wide), BF16),
            vm((1, keys_wide), F32),
            vm((halves, REACH, part, wide), BF16),
            vm((REACH, 1, keys_wide), F32),
            vm((part, wide), F32),
            vm((halves, slots, part, wide), BF16),
            vm((halves, DV, wide), BF16),
            dma((halves, slots)), dma((halves, slots)),
            dma((slots,)), dma((slots,)),
            dma((halves, REACH)), dma((halves, REACH)),
            dma((REACH,)), dma((REACH,)),
            dma((halves, slots)), dma((halves, slots)),
            dma((5,)), dma((5,)),
            dma((5, 2)), dma((5, 2)),
            dma((5, 2)), dma((5, 2)),
            dma((5, 5)), dma((5, 5)),
            dma((chunks,)), dma((chunks,)),
            dma((chunks,)), dma((chunks,)),
            dma((8,)),
        ],
        compiler_params=pltpu.CompilerParams(
            collective_id=0, has_side_effects=True, vmem_limit_bytes=58 * 2**20
        ),
    )(segment_ids, log_gate, keys, values, queries, out_gate, final_projector)
    return pl.pallas_call(
        copy_kernel,
        in_specs=[pl.BlockSpec(memory_space=pltpu.VMEM)],
        out_specs=pl.BlockSpec(memory_space=pl.ANY),
        out_shape=jax.ShapeDtypeStruct((tokens, width), BF16),
        scratch_shapes=[dma((4,))],
        compiler_params=pltpu.CompilerParams(vmem_limit_bytes=16 * 2**20),
    )(projected)


def solution(mesh):
    return jax.shard_map(
        shards,
        mesh=mesh,
        in_specs=(
            P("ctx", "head"),
            P("ctx", "head"),
            P("ctx", "head"),
            P("ctx", "head"),
            P("ctx", "head"),
            P(),
            P("head", None),
        ),
        out_specs=P("ctx", "head"),
        check_vma=False,
    )
```

```python
import jax
import jax.numpy as jnp
from jax import lax
from jax.experimental import pallas as pl
from jax.experimental.pallas import tpu as pltpu
from jax.sharding import PartitionSpec as P

DK = 128
DV = 256
CH = 128
F32 = jnp.float32
BF16 = jnp.bfloat16
MESH = pl.DeviceIdType.MESH

NX = 4
FAR_FIRST = (4, 3, 5, 2, 6, 1, 7)
NZ = 8
PIECE = 64
CROSS = 2
REACH = 4


def dot(a, b, dims):
    return lax.dot_general(a, b, (dims, ((), ())), preferred_element_type=F32)


def layer_kernel(
    seg, g_h, k_h, v_h, q_h, gate_h, proj_h, out,
    g, k, v, q, cum, state_f, state, starts, weights, decay, weight_now,
    mixed, reach, gate, wo, wp, hid, hid_peer, send, recv, own, ahead_of,
    p1, a1, xs, acc, t_out, a_out, t_in, a_in, plane, p3, e_in,
    s_p1, r_p1, s_a1, r_a1, s_p2, r_p2, s_a2, r_a2, s_p3, r_p3,
    s_w1, r_w1, s_wx, r_wx, s_wf, r_wf, s_ws, r_ws,
    s_hid, r_hid, s_rs, r_rs, s_load,
):
    ctx = lax.axis_index("ctx")
    y = lax.axis_index("head")
    z = ctx // (2 * NX)
    me = ctx % (2 * NX)
    x = me // 2
    core = me % 2
    base = z * (2 * NX)
    pair = y + 1 - 2 * (y % 2)
    over = 3 - y
    over_pair = over + 1 - 2 * (over % 2)
    xr = (x + 1) % NX
    xl = (x + NX - 1) % NX
    xo = (x + 2) % NX
    tokens = hid.shape[0]
    blocks = tokens // CH
    chunks = tokens // PIECE
    heads = reach.shape[1] // DK
    width = wo.shape[2]
    depth = wo.shape[1]
    slab = depth // (2 * NX)
    part = p1.shape[2]

    def rdma(src, dst, ssem, rsem, c, h):
        return pltpu.make_async_remote_copy(
            src_ref=src, dst_ref=dst, send_sem=ssem, recv_sem=rsem,
            device_id={"ctx": c, "head": h}, device_id_type=MESH,
        )

    def arrived(dst, ssem, rsem):
        rdma(dst, dst, ssem, rsem, ctx, pair).wait_recv()

    def left(src, ssem, rsem):
        rdma(src, src, ssem, rsem, ctx, pair).wait_send()

    mine_cols = pl.ds(pl.multiple_of(y * width, width), width)
    over_cols = pl.ds(pl.multiple_of(over * width, width), width)
    pair_cols = pl.ds(pl.multiple_of(pair * width, width), width)
    loads = [
        pltpu.make_async_copy(src, dst, s_load.at[i])
        for i, (src, dst) in enumerate(
            (
                (g_h, g), (k_h, k), (v_h, v), (q_h, q), (gate_h, gate),
                (proj_h.at[:, over_cols], wo.at[1]), (proj_h.at[:, mine_cols], wo.at[0]),
                (proj_h.at[:, pair_cols], wo.at[2]),
            )
        )
    ]
    for load in loads[:3]:
        load.start()

    barrier = pltpu.get_barrier_semaphore()

    def greet(c, h):
        pl.semaphore_signal(barrier, inc=1, device_id={"ctx": c, "head": h}, device_id_type=MESH)

    greet(ctx, pair)
    greet(ctx, over)
    for step in range(1, 2 * NX):
        greet(base + (me + step) % (2 * NX), y)
    for far in range(1, REACH + 1):

        @pl.when(z + far < NZ)
        def _():
            greet(ctx + far * 2 * NX, y)

        @pl.when(z - far >= 0)
        def _():
            greet(ctx - far * 2 * NX, y)

    ahead = jnp.minimum(NZ - 1 - z, REACH)
    behind = jnp.minimum(z, REACH)
    pl.semaphore_wait(barrier, 2 * NX + 1 + ahead + behind)

    units = (
        (1, 0, slab // 2, pair, 3 - pair),
        (1, slab // 2, slab // 2, pair, 3 - pair),
        (0, 0, slab, pair, pair),
        (3, 0, slab, over, over_pair),
        (2, 0, slab, over, over),
    )

    def unit_rows(u, xx, cc, half=None):
        _, first, size, _, _ = units[u]
        if half is not None:
            size = size // 2
            first = first + half * size
        return pl.ds(pl.multiple_of((xx * 2 + cc) * slab + first, size), size)

    at_r = base + xr * 2 + core
    at_l = base + xl * 2 + core
    sib = base + x * 2 + 1 - core

    def w1(u):
        j, _, _, to, block = units[u]
        rows = unit_rows(u, x, core)
        cols = pl.ds(pl.multiple_of(block * width, width), width)
        return rdma(proj_h.at[rows, cols], wp.at[j, rows], s_w1.at[u], r_w1.at[u], ctx, to)

    def along(u, rows, s, r, item, to):
        j = units[u][0]
        return rdma(wp.at[j, rows], wp.at[j, rows], s.at[u, item], r.at[u, item], to, y)

    def wait_in(u, rows, s, r, item):
        arrived(wp.at[units[u][0], rows], s.at[u, item], r.at[u, item])

    def relays(u, cc):
        return (
            unit_rows(u, x, cc), unit_rows(u, xl, cc), unit_rows(u, xr, cc),
            unit_rows(u, xo, cc, 0), unit_rows(u, xo, cc, 1),
        )

    def stage_a(u):
        here = unit_rows(u, x, core)
        arrived(wp.at[units[u][0], here], s_w1.at[u], r_w1.at[u])
        along(u, here, s_wx, r_wx, 0, at_r).start()
        along(u, here, s_wx, r_wx, 1, at_l).start()
        along(u, here, s_ws, r_ws, 0, sib).start()

    def stage_b(u):
        wait_in(u, unit_rows(u, xl, core), s_wx, r_wx, 0)
        along(u, unit_rows(u, xl, core, 0), s_wf, r_wf, 0, at_r).start()
        along(u, unit_rows(u, xl, core), s_ws, r_ws, 1, sib).start()
        wait_in(u, unit_rows(u, xr, core), s_wx, r_wx, 1)
        along(u, unit_rows(u, xr, core, 1), s_wf, r_wf, 1, at_l).start()
        along(u, unit_rows(u, xr, core), s_ws, r_ws, 2, sib).start()

    def stage_c(u):
        wait_in(u, unit_rows(u, xo, core, 0), s_wf, r_wf, 0)
        along(u, unit_rows(u, xo, core, 0), s_ws, r_ws, 3, sib).start()
        wait_in(u, unit_rows(u, xo, core, 1), s_wf, r_wf, 1)
        along(u, unit_rows(u, xo, core, 1), s_ws, r_ws, 4, sib).start()

    def stage_d(u):
        for item, rows in enumerate(relays(u, 1 - core)):
            wait_in(u, rows, s_ws, r_ws, item)

    def weights_left(u):
        j = units[u][0]
        here = unit_rows(u, x, core)
        left(wp.at[j, here], s_w1.at[u], r_w1.at[u])
        for item in range(2):
            left(wp.at[j, here], s_wx.at[u, item], r_wx.at[u, item])
            left(wp.at[j, unit_rows(u, x, core, 0)], s_wf.at[u, item], r_wf.at[u, item])
        for item, rows in enumerate(relays(u, core)):
            left(wp.at[j, rows], s_ws.at[u, item], r_ws.at[u, item])

    for u in (0, 1, 3, 4):
        w1(u).start()

    block_rows = lax.broadcasted_iota(jnp.int32, (CH, CH), 0)
    block_cols = lax.broadcasted_iota(jnp.int32, (CH, CH), 1)
    causal = block_cols <= block_rows
    ones = causal.astype(F32).astype(BF16)
    state_f[...] = jnp.zeros_like(state_f)
    weight_now[...] = jnp.ones_like(weight_now)
    wide = p1.shape[3]
    halves = p1.shape[0]
    group = heads // halves

    def rows_at(c, size):
        return pl.ds(pl.multiple_of(c * size, size), size)

    def head_keys(h):
        return slice(h * DK, (h + 1) * DK)

    def head_vals(h):
        return slice(h * DV, (h + 1) * DV)

    for load in loads[:3]:
        load.wait()
    for load in loads[3:]:
        load.start()

    def same_stream(b):
        at = ctx * blocks + b
        same = jnp.logical_and(seg[at] == seg[jnp.maximum(at - 1, 0)], at > 0)
        return jnp.where(same, 1.0, 0.0)

    def state_step(f, b):
        lanes = slice(f * wide, (f + 1) * wide)
        rows = rows_at(b, CH)
        keep = same_stream(b)
        sums = dot(ones, g[rows, lanes], ((1,), (0,)))
        cum[rows, lanes] = sums
        last = sums[CH - 1 : CH, :]
        kept = (k[rows, lanes].astype(F32) * jnp.exp(last - sums)).astype(BF16)
        fall = jnp.exp(last)
        weight = weight_now[f] * keep
        weights[b, :, lanes] = weight
        weight_now[f] = weight * fall
        for i in range(group):
            kc = head_keys(i)
            start = state_f[f, :, kc] * keep
            starts[b, :, head_keys(f * group + i)] = start.astype(BF16)
            added = dot(v[rows, head_vals(f * group + i)], kept[:, kc], ((0,), (0,)))
            state_f[f, :, kc] = start * fall[:, kc] + added

    def rows_of(i):
        return pl.ds(pl.multiple_of(i * part, part), part)

    for f in range(halves):

        def step_of(b, carry):
            state_step(f, b)
            return carry

        lax.fori_loop(0, blocks, step_of, 0, unroll=8)
        state[f] = state_f[f].astype(BF16)
        for step in FAR_FIRST:
            i = (me + step) % (2 * NX)
            rdma(
                state.at[f, rows_of(i), :], p1.at[f, me], s_p1.at[f, i], r_p1.at[f, me], base + i, y
            ).start()
        p1[f, me] = state[f, rows_of(me), :]

        if f == 0:
            flags = [same_stream(b) for b in range(blocks)]
            through = flags[0]
            for flag in flags[1:]:
                through = through * flag
            total = dot(jnp.ones((16, tokens), BF16), g[...], ((1,), (0,)))[:1]
            decay[...] = jnp.exp(total) * through
            for step in range(1, 2 * NX):
                i = (me + step) % (2 * NX)
                rdma(decay, a1.at[me], s_a1.at[i], r_a1.at[me], base + i, y).start()
            a1[me] = decay[...]

    def block_step(b, carry):
        rows = rows_at(b, CH)
        sums = cum[rows, :]
        dq = q[rows, :].astype(F32) * jnp.exp(sums) * DK ** (-0.5)
        dk = (k[rows, :].astype(F32) * jnp.exp(-sums)).astype(BF16)
        reach[rows, :] = (dq * weights[b]).astype(BF16)
        dq = dq.astype(BF16)
        for h in range(heads):
            kc = head_keys(h)
            vc = head_vals(h)
            scores = dot(dq[:, kc], dk[:, kc], ((1,), (1,)))
            probs = jnp.where(causal, scores, 0.0).astype(BF16)
            out = dot(probs, v[rows, vc], ((1,), (0,)))
            out += dot(dq[:, kc], starts[b, :, kc], ((1,), (1,)))
            mixed[rows, vc] = out.astype(BF16)
        return carry

    loads[3].wait()
    first_part = 3
    lax.fori_loop(0, first_part, block_step, 0, unroll=first_part)


    for step in range(1, 2 * NX):
        i = (me + step) % (2 * NX)
        arrived(a1.at[i], s_a1.at[i], r_a1.at[i])
    scale = jnp.ones_like(decay[...])
    for i in range(2 * NX):
        acc[i] = scale
        scale = scale * a1[i]
    a_out[...] = scale
    for far in range(1, REACH + 1):

        @pl.when(z + far < NZ)
        def _():
            n = far - 1
            rdma(a_out, a_in.at[n], s_a2.at[n], r_a2.at[n], ctx + far * 2 * NX, y).start()

    for f in range(halves):
        for step in range(1, 2 * NX):
            i = (me + step) % (2 * NX)
            arrived(p1.at[f, i], s_p1.at[f, i], r_p1.at[f, i])
        run = jnp.zeros((part, wide), F32)
        lanes = slice(f * wide, (f + 1) * wide)
        for i in range(2 * NX):
            xs[f, i] = run
            run = run * a1[i, :, lanes] + p1[f, i].astype(F32)
        t_out[f] = run.astype(BF16)
        for far in range(REACH, 0, -1):

            @pl.when(z + far < NZ)
            def _():
                to = ctx + far * 2 * NX
                n = far - 1
                rdma(t_out.at[f], t_in.at[f, n], s_p2.at[f, n], r_p2.at[f, n], to, y).start()

        stage_a(f)

    w1(2).start()
    lax.fori_loop(first_part, blocks, block_step, 0, unroll=blocks - first_part)

    for f in range(halves):
        lanes = slice(f * wide, (f + 1) * wide)
        plane[...] = jnp.zeros_like(plane)
        for far in range(REACH, 0, -1):

            @pl.when(z - far >= 0)
            def _():
                n = far - 1
                if f == 0:
                    arrived(a_in.at[n], s_a2.at[n], r_a2.at[n])
                arrived(t_in.at[f, n], s_p2.at[f, n], r_p2.at[f, n])
                plane[...] = plane[...] * a_in[n, :, lanes] + t_in[f, n].astype(F32)

        for i in range(2 * NX):
            p3[f, i] = (xs[f, i] + acc[i, :, lanes] * plane[...]).astype(BF16)
        for step in FAR_FIRST:
            i = (me + step) % (2 * NX)
            rdma(
                p3.at[f, i], e_in.at[f, rows_of(me), :], s_p3.at[f, i], r_p3.at[f, me], base + i, y
            ).start()
        e_in[f, rows_of(me), :] = p3[f, me]

    stage_b(0)
    stage_b(1)
    loads[4].wait()

    for f in range(halves):
        for step in range(1, 2 * NX):
            i = (me + step) % (2 * NX)
            arrived(e_in.at[f, rows_of(i), :], s_p3.at[f, i], r_p3.at[f, i])

    straight = chunks - CROSS

    def hidden_step(step, carry):
        c = jnp.where(step < 2 * CROSS, step // 2 + (step % 2) * straight, step - CROSS)
        to = jnp.where(c < straight, pair, over)
        rows = rows_at(c, PIECE)
        for h in range(heads):
            kc = head_keys(h)
            vc = head_vals(h)
            full = mixed[rows, vc].astype(F32)
            full += dot(reach[rows, kc], e_in[h // group, :, head_keys(h % group)], ((1,), (1,)))
            mean = jnp.mean(full * full, axis=-1, keepdims=True)
            val = gate[rows, vc].astype(F32)
            silu = val / (1.0 + jnp.exp(-val))
            hid[rows, vc] = (full * lax.rsqrt(mean + 1e-5) * silu).astype(BF16)
        rdma(hid.at[rows, :], hid_peer.at[rows, :], s_hid.at[c], r_hid.at[c], ctx, to).start()
        return carry

    lax.fori_loop(0, 2 * CROSS, hidden_step, 0)
    stage_c(0)
    lax.fori_loop(2 * CROSS, chunks, hidden_step, 0)

    stage_c(1)
    stage_a(2)
    for load in loads[5:]:
        load.wait()
    stage_d(0)
    stage_d(1)

    tile = 512

    def columns(do):
        def column(n, carry):
            do(pl.ds(pl.multiple_of(n * tile, tile), tile))
            return carry

        lax.fori_loop(0, width // tile, column, 0)

    def own_sums(first, count, j):
        rows = pl.ds(first * PIECE, count * PIECE)

        def both_parts(cols):
            total = dot(hid[rows, :], wo[0, :, cols], ((1,), (0,)))
            own[rows, cols] = total + dot(hid_peer[rows, :], wp[j, :, cols], ((1,), (0,)))

        columns(both_parts)

    def piece_at(step):
        late = step - (chunks - 2 * CROSS + 1)
        crossed = jnp.logical_and(late >= 0, late % 2 == 0)
        behind_cross = step - (late + 1) // 2
        return jnp.where(late < 0, step, jnp.where(crossed, straight + late // 2, behind_cross))

    def main_step(step, carry):
        c = piece_at(step)
        crossed = c >= straight
        to = jnp.where(crossed, pair, over)
        jo = jnp.where(crossed, 2, 1)
        jp = jnp.where(crossed, 3, 1)
        rows = rows_at(c, PIECE)

        def own_part(cols):
            ahead_of[:, cols] = dot(hid[rows, :], wo[jo, :, cols], ((1,), (0,)))

        def pair_part(cols):
            total = ahead_of[:, cols] + dot(hid_peer[rows, :], wp[jp, :, cols], ((1,), (0,)))
            send[rows, cols] = total.astype(BF16)

        columns(own_part)
        arrived(hid_peer.at[rows, :], s_hid.at[c], r_hid.at[c])
        columns(pair_part)
        rdma(send.at[rows, :], recv.at[rows, :], s_rs.at[c], r_rs.at[c], ctx, to).start()

        def at(when, *actions):
            @pl.when(step == when)
            def _():
                for action, *args in actions:
                    action(*args)

        at(3, (stage_b, 2), (stage_a, 3))
        at(5, (stage_c, 2))
        at(6, (stage_b, 3), (stage_a, 4))
        at(7, (stage_d, 2), (own_sums, 0, 4, 0))
        at(8, (stage_c, 3))
        at(9, (own_sums, 4, 4, 0))
        at(10, (stage_d, 3))
        at(11, (stage_b, 4), (own_sums, 8, 4, 0))
        at(14, (stage_c, 4))
        return carry

    lax.fori_loop(0, chunks, main_step, 0)
    stage_d(4)
    own_sums(12, straight - 12, 0)
    own_sums(straight, CROSS, 2)

    for f in range(halves):
        for step in range(1, 2 * NX):
            i = (me + step) % (2 * NX)
            if f == 0:
                left(decay, s_a1.at[i], r_a1.at[i])
            left(p1.at[f, i], s_p1.at[f, i], r_p1.at[f, i])
            left(p3.at[f, i], s_p3.at[f, i], r_p3.at[f, i])
        for far in range(1, REACH + 1):

            @pl.when(z + far < NZ)
            def _():
                n = far - 1
                if f == 0:
                    left(a_out, s_a2.at[n], r_a2.at[n])
                left(t_out.at[f], s_p2.at[f, n], r_p2.at[f, n])

    for u in range(len(units)):
        weights_left(u)

    def hidden_left(c, carry):
        rows = rows_at(c, PIECE)
        left(hid.at[rows, :], s_hid.at[c], r_hid.at[c])
        return carry

    lax.fori_loop(0, chunks, hidden_left, 0)

    def result_step(step, carry):
        c = piece_at(step)
        rows = rows_at(c, PIECE)
        arrived(recv.at[rows, :], s_rs.at[c], r_rs.at[c])
        out[rows, :] = (own[rows, :] + recv[rows, :].astype(F32)).astype(BF16)

        @pl.when(step >= 2)
        def _():
            before = piece_at(step - 2)
            left(send.at[rows_at(before, PIECE), :], s_rs.at[before], r_rs.at[before])

        return carry

    lax.fori_loop(0, chunks, result_step, 0)
    for step in range(chunks - 2, chunks):
        left(send.at[rows_at(piece_at(step), PIECE), :], s_rs.at[piece_at(step)], r_rs.at[piece_at(step)])


def copy_kernel(src, dst, sems):
    parts = sems.shape[0]
    size = src.shape[0] // parts
    writes = [
        pltpu.make_async_copy(src.at[pl.ds(i * size, size)], dst.at[pl.ds(i * size, size)], sems.at[i])
        for i in range(parts)
    ]
    for write in writes:
        write.start()
    for write in writes:
        write.wait()


def shards(queries, keys, values, log_gate, out_gate, segment_ids, final_projector):
    tokens = queries.shape[0]
    keys_wide = queries.shape[1]
    vals_wide = values.shape[1]
    depth, full = final_projector.shape
    width = full // 4
    slots = 2 * NX
    part = DV // slots
    blocks = tokens // CH
    chunks = tokens // PIECE
    halves = 2
    wide = keys_wide // halves

    vm = pltpu.VMEM
    dma = pltpu.SemaphoreType.DMA
    projected = pl.pallas_call(
        layer_kernel,
        in_specs=[pl.BlockSpec(memory_space=pltpu.SMEM)] + [pl.BlockSpec(memory_space=pl.ANY)] * 6,
        out_specs=pl.BlockSpec(memory_space=pltpu.VMEM),
        out_shape=pltpu.VMEM((tokens, width), BF16),
        scratch_shapes=[
            vm((tokens, keys_wide), BF16),
            vm((tokens, keys_wide), BF16),
            vm((tokens, vals_wide), BF16),
            vm((tokens, keys_wide), BF16),
            vm((tokens, keys_wide), F32),
            vm((halves, DV, wide), F32),
            vm((halves, DV, wide), BF16),
            vm((blocks, DV, keys_wide), BF16),
            vm((blocks, 1, keys_wide), F32),
            vm((1, keys_wide), F32),
            vm((halves, 1, wide), F32),
            vm((tokens, vals_wide), BF16),
            vm((tokens, keys_wide), BF16),
            vm((tokens, vals_wide), BF16),
            vm((3, depth, width), BF16),
            vm((4, depth, width), BF16),
            vm((tokens, vals_wide), BF16),
            vm((tokens, vals_wide), BF16),
            vm((tokens, width), BF16),
            vm((tokens, width), BF16),
            vm((tokens, width), F32),
            vm((PIECE, width), F32),
            vm((halves, slots, part, wide), BF16),
            vm((slots, 1, keys_wide), F32),
            vm((halves, slots, part, wide), F32),
            vm((slots, 1, keys_wide), F32),
            vm((halves, part, wide), BF16),
            vm((1, keys_wide), F32),
            vm((halves, REACH, part, wide), BF16),
            vm((REACH, 1, keys_wide), F32),
            vm((part, wide), F32),
            vm((halves, slots, part, wide), BF16),
            vm((halves, DV, wide), BF16),
            dma((halves, slots)), dma((halves, slots)),
            dma((slots,)), dma((slots,)),
            dma((halves, REACH)), dma((halves, REACH)),
            dma((REACH,)), dma((REACH,)),
            dma((halves, slots)), dma((halves, slots)),
            dma((5,)), dma((5,)),
            dma((5, 2)), dma((5, 2)),
            dma((5, 2)), dma((5, 2)),
            dma((5, 5)), dma((5, 5)),
            dma((chunks,)), dma((chunks,)),
            dma((chunks,)), dma((chunks,)),
            dma((8,)),
        ],
        compiler_params=pltpu.CompilerParams(
            collective_id=0, has_side_effects=True, vmem_limit_bytes=58 * 2**20
        ),
    )(segment_ids, log_gate, keys, values, queries, out_gate, final_projector)
    return pl.pallas_call(
        copy_kernel,
        in_specs=[pl.BlockSpec(memory_space=pltpu.VMEM)],
        out_specs=pl.BlockSpec(memory_space=pl.ANY),
        out_shape=jax.ShapeDtypeStruct((tokens, width), BF16),
        scratch_shapes=[dma((4,))],
        compiler_params=pltpu.CompilerParams(vmem_limit_bytes=16 * 2**20),
    )(projected)


def solution(mesh):
    return jax.shard_map(
        shards,
        mesh=mesh,
        in_specs=(
            P("ctx", "head"),
            P("ctx", "head"),
            P("ctx", "head"),
            P("ctx", "head"),
            P("ctx", "head"),
            P(),
            P("head", None),
        ),
        out_specs=P("ctx", "head"),
        check_vma=False,
    )
```

```python
import jax
import jax.numpy as jnp
from jax import lax
from jax.experimental import pallas as pl
from jax.experimental.pallas import tpu as pltpu
from jax.sharding import PartitionSpec as P

DK = 128
DV = 256
CH = 128
F32 = jnp.float32
BF16 = jnp.bfloat16
MESH = pl.DeviceIdType.MESH

NX = 4
FAR_FIRST = (4, 3, 5, 2, 6, 1, 7)
NZ = 8
PIECE = 64
CROSS = 2
REACH = 4


def dot(a, b, dims):
    return lax.dot_general(a, b, (dims, ((), ())), preferred_element_type=F32)


def layer_kernel(
    seg, g_h, k_h, v_h, q_h, gate_h, proj_h, out,
    g, k, v, q, cum, state_f, state, starts, weights, decay, weight_now,
    mixed, reach, gate, wo, wp, hid, hid_peer, send, recv, own, ahead_of,
    p1, a1, xs, acc, t_out, a_out, t_in, a_in, plane, p3, e_in,
    s_p1, r_p1, s_a1, r_a1, s_p2, r_p2, s_a2, r_a2, s_p3, r_p3,
    s_w1, r_w1, s_wx, r_wx, s_wf, r_wf, s_ws, r_ws,
    s_hid, r_hid, s_rs, r_rs, s_load,
):
    ctx = lax.axis_index("ctx")
    y = lax.axis_index("head")
    z = ctx // (2 * NX)
    me = ctx % (2 * NX)
    x = me // 2
    core = me % 2
    base = z * (2 * NX)
    pair = y + 1 - 2 * (y % 2)
    over = 3 - y
    over_pair = over + 1 - 2 * (over % 2)
    xr = (x + 1) % NX
    xl = (x + NX - 1) % NX
    xo = (x + 2) % NX
    tokens = hid.shape[0]
    blocks = tokens // CH
    chunks = tokens // PIECE
    heads = reach.shape[1] // DK
    width = wo.shape[2]
    depth = wo.shape[1]
    slab = depth // (2 * NX)
    part = p1.shape[2]

    def rdma(src, dst, ssem, rsem, c, h):
        return pltpu.make_async_remote_copy(
            src_ref=src, dst_ref=dst, send_sem=ssem, recv_sem=rsem,
            device_id={"ctx": c, "head": h}, device_id_type=MESH,
        )

    def arrived(dst, ssem, rsem):
        rdma(dst, dst, ssem, rsem, ctx, pair).wait_recv()

    def left(src, ssem, rsem):
        rdma(src, src, ssem, rsem, ctx, pair).wait_send()

    mine_cols = pl.ds(pl.multiple_of(y * width, width), width)
    over_cols = pl.ds(pl.multiple_of(over * width, width), width)
    pair_cols = pl.ds(pl.multiple_of(pair * width, width), width)
    loads = [
        pltpu.make_async_copy(src, dst, s_load.at[i])
        for i, (src, dst) in enumerate(
            (
                (g_h, g), (k_h, k), (v_h, v), (q_h, q), (gate_h, gate),
                (proj_h.at[:, over_cols], wo.at[1]), (proj_h.at[:, mine_cols], wo.at[0]),
                (proj_h.at[:, pair_cols], wo.at[2]),
            )
        )
    ]
    for load in loads[:3]:
        load.start()

    barrier = pltpu.get_barrier_semaphore()

    def greet(c, h):
        pl.semaphore_signal(barrier, inc=1, device_id={"ctx": c, "head": h}, device_id_type=MESH)

    greet(ctx, pair)
    greet(ctx, over)
    for step in range(1, 2 * NX):
        greet(base + (me + step) % (2 * NX), y)
    for far in range(1, REACH + 1):

        @pl.when(z + far < NZ)
        def _():
            greet(ctx + far * 2 * NX, y)

        @pl.when(z - far >= 0)
        def _():
            greet(ctx - far * 2 * NX, y)

    ahead = jnp.minimum(NZ - 1 - z, REACH)
    behind = jnp.minimum(z, REACH)
    pl.semaphore_wait(barrier, 2 * NX + 1 + ahead + behind)

    units = (
        (1, 0, slab // 2, pair, 3 - pair),
        (1, slab // 2, slab // 2, pair, 3 - pair),
        (0, 0, slab, pair, pair),
        (3, 0, slab, over, over_pair),
        (2, 0, slab, over, over),
    )

    def unit_rows(u, xx, cc, half=None):
        _, first, size, _, _ = units[u]
        if half is not None:
            size = size // 2
            first = first + half * size
        return pl.ds(pl.multiple_of((xx * 2 + cc) * slab + first, size), size)

    at_r = base + xr * 2 + core
    at_l = base + xl * 2 + core
    sib = base + x * 2 + 1 - core

    def w1(u):
        j, _, _, to, block = units[u]
        rows = unit_rows(u, x, core)
        cols = pl.ds(pl.multiple_of(block * width, width), width)
        return rdma(proj_h.at[rows, cols], wp.at[j, rows], s_w1.at[u], r_w1.at[u], ctx, to)

    def along(u, rows, s, r, item, to):
        j = units[u][0]
        return rdma(wp.at[j, rows], wp.at[j, rows], s.at[u, item], r.at[u, item], to, y)

    def wait_in(u, rows, s, r, item):
        arrived(wp.at[units[u][0], rows], s.at[u, item], r.at[u, item])

    def relays(u, cc):
        return (
            unit_rows(u, x, cc), unit_rows(u, xl, cc), unit_rows(u, xr, cc),
            unit_rows(u, xo, cc, 0), unit_rows(u, xo, cc, 1),
        )

    def stage_a(u):
        here = unit_rows(u, x, core)
        arrived(wp.at[units[u][0], here], s_w1.at[u], r_w1.at[u])
        along(u, here, s_wx, r_wx, 0, at_r).start()
        along(u, here, s_wx, r_wx, 1, at_l).start()
        along(u, here, s_ws, r_ws, 0, sib).start()

    def stage_b(u):
        wait_in(u, unit_rows(u, xl, core), s_wx, r_wx, 0)
        along(u, unit_rows(u, xl, core, 0), s_wf, r_wf, 0, at_r).start()
        along(u, unit_rows(u, xl, core), s_ws, r_ws, 1, sib).start()
        wait_in(u, unit_rows(u, xr, core), s_wx, r_wx, 1)
        along(u, unit_rows(u, xr, core, 1), s_wf, r_wf, 1, at_l).start()
        along(u, unit_rows(u, xr, core), s_ws, r_ws, 2, sib).start()

    def stage_c(u):
        wait_in(u, unit_rows(u, xo, core, 0), s_wf, r_wf, 0)
        along(u, unit_rows(u, xo, core, 0), s_ws, r_ws, 3, sib).start()
        wait_in(u, unit_rows(u, xo, core, 1), s_wf, r_wf, 1)
        along(u, unit_rows(u, xo, core, 1), s_ws, r_ws, 4, sib).start()

    def stage_d(u):
        for item, rows in enumerate(relays(u, 1 - core)):
            wait_in(u, rows, s_ws, r_ws, item)

    def weights_left(u):
        j = units[u][0]
        here = unit_rows(u, x, core)
        left(wp.at[j, here], s_w1.at[u], r_w1.at[u])
        for item in range(2):
            left(wp.at[j, here], s_wx.at[u, item], r_wx.at[u, item])
            left(wp.at[j, unit_rows(u, x, core, 0)], s_wf.at[u, item], r_wf.at[u, item])
        for item, rows in enumerate(relays(u, core)):
            left(wp.at[j, rows], s_ws.at[u, item], r_ws.at[u, item])

    for u in (0, 1, 3, 4):
        w1(u).start()

    block_rows = lax.broadcasted_iota(jnp.int32, (CH, CH), 0)
    block_cols = lax.broadcasted_iota(jnp.int32, (CH, CH), 1)
    causal = block_cols <= block_rows
    ones = causal.astype(F32).astype(BF16)
    state_f[...] = jnp.zeros_like(state_f)
    weight_now[...] = jnp.ones_like(weight_now)
    wide = p1.shape[3]
    halves = p1.shape[0]
    group = heads // halves

    def rows_at(c, size):
        return pl.ds(pl.multiple_of(c * size, size), size)

    def head_keys(h):
        return slice(h * DK, (h + 1) * DK)

    def head_vals(h):
        return slice(h * DV, (h + 1) * DV)

    for load in loads[:3]:
        load.wait()
    for load in loads[3:]:
        load.start()

    def same_stream(b):
        at = ctx * blocks + b
        same = jnp.logical_and(seg[at] == seg[jnp.maximum(at - 1, 0)], at > 0)
        return jnp.where(same, 1.0, 0.0)

    def state_step(f, b):
        lanes = slice(f * wide, (f + 1) * wide)
        rows = rows_at(b, CH)
        keep = same_stream(b)
        sums = dot(ones, g[rows, lanes], ((1,), (0,)))
        cum[rows, lanes] = sums
        last = sums[CH - 1 : CH, :]
        kept = (k[rows, lanes].astype(F32) * jnp.exp(last - sums)).astype(BF16)
        fall = jnp.exp(last)
        weight = weight_now[f] * keep
        weights[b, :, lanes] = weight
        weight_now[f] = weight * fall
        for i in range(group):
            kc = head_keys(i)
            start = state_f[f, :, kc] * keep
            starts[b, :, head_keys(f * group + i)] = start.astype(BF16)
            added = dot(v[rows, head_vals(f * group + i)], kept[:, kc], ((0,), (0,)))
            state_f[f, :, kc] = start * fall[:, kc] + added

    def rows_of(i):
        return pl.ds(pl.multiple_of(i * part, part), part)

    for f in range(halves):

        def step_of(b, carry):
            state_step(f, b)
            return carry

        lax.fori_loop(0, blocks, step_of, 0, unroll=8)
        state[f] = state_f[f].astype(BF16)
        for step in FAR_FIRST:
            i = (me + step) % (2 * NX)
            rdma(
                state.at[f, rows_of(i), :], p1.at[f, me], s_p1.at[f, i], r_p1.at[f, me], base + i, y
            ).start()
        p1[f, me] = state[f, rows_of(me), :]

        if f == 0:
            flags = [same_stream(b) for b in range(blocks)]
            through = flags[0]
            for flag in flags[1:]:
                through = through * flag
            total = dot(jnp.ones((16, tokens), BF16), g[...], ((1,), (0,)))[:1]
            decay[...] = jnp.exp(total) * through
            for step in range(1, 2 * NX):
                i = (me + step) % (2 * NX)
                rdma(decay, a1.at[me], s_a1.at[i], r_a1.at[me], base + i, y).start()
            a1[me] = decay[...]

    def block_step(b, carry):
        rows = rows_at(b, CH)
        sums = cum[rows, :]
        dq = q[rows, :].astype(F32) * jnp.exp(sums) * DK ** (-0.5)
        dk = (k[rows, :].astype(F32) * jnp.exp(-sums)).astype(BF16)
        reach[rows, :] = (dq * weights[b]).astype(BF16)
        dq = dq.astype(BF16)
        for h in range(heads):
            kc = head_keys(h)
            vc = head_vals(h)
            scores = dot(dq[:, kc], dk[:, kc], ((1,), (1,)))
            probs = jnp.where(causal, scores, 0.0).astype(BF16)
            out = dot(probs, v[rows, vc], ((1,), (0,)))
            out += dot(dq[:, kc], starts[b, :, kc], ((1,), (1,)))
            mixed[rows, vc] = out.astype(BF16)
        return carry

    loads[3].wait()
    first_part = 3
    lax.fori_loop(0, first_part, block_step, 0, unroll=first_part)


    for step in range(1, 2 * NX):
        i = (me + step) % (2 * NX)
        arrived(a1.at[i], s_a1.at[i], r_a1.at[i])
    scale = jnp.ones_like(decay[...])
    for i in range(2 * NX):
        acc[i] = scale
        scale = scale * a1[i]
    a_out[...] = scale
    for far in range(1, REACH + 1):

        @pl.when(z + far < NZ)
        def _():
            n = far - 1
            rdma(a_out, a_in.at[n], s_a2.at[n], r_a2.at[n], ctx + far * 2 * NX, y).start()

    for f in range(halves):
        for step in range(1, 2 * NX):
            i = (me + step) % (2 * NX)
            arrived(p1.at[f, i], s_p1.at[f, i], r_p1.at[f, i])
        run = jnp.zeros((part, wide), F32)
        lanes = slice(f * wide, (f + 1) * wide)
        for i in range(2 * NX):
            xs[f, i] = run
            run = run * a1[i, :, lanes] + p1[f, i].astype(F32)
        t_out[f] = run.astype(BF16)
        for far in range(REACH, 0, -1):

            @pl.when(z + far < NZ)
            def _():
                to = ctx + far * 2 * NX
                n = far - 1
                rdma(t_out.at[f], t_in.at[f, n], s_p2.at[f, n], r_p2.at[f, n], to, y).start()

        stage_a(f)

    w1(2).start()
    lax.fori_loop(first_part, blocks, block_step, 0, unroll=blocks - first_part)

    for f in range(halves):
        lanes = slice(f * wide, (f + 1) * wide)
        plane[...] = jnp.zeros_like(plane)
        for far in range(REACH, 0, -1):

            @pl.when(z - far >= 0)
            def _():
                n = far - 1
                if f == 0:
                    arrived(a_in.at[n], s_a2.at[n], r_a2.at[n])
                arrived(t_in.at[f, n], s_p2.at[f, n], r_p2.at[f, n])
                plane[...] = plane[...] * a_in[n, :, lanes] + t_in[f, n].astype(F32)

        for i in range(2 * NX):
            p3[f, i] = (xs[f, i] + acc[i, :, lanes] * plane[...]).astype(BF16)
        for step in FAR_FIRST:
            i = (me + step) % (2 * NX)
            rdma(
                p3.at[f, i], e_in.at[f, rows_of(me), :], s_p3.at[f, i], r_p3.at[f, me], base + i, y
            ).start()
        e_in[f, rows_of(me), :] = p3[f, me]

    stage_b(0)
    stage_b(1)
    loads[4].wait()

    for f in range(halves):
        for step in range(1, 2 * NX):
            i = (me + step) % (2 * NX)
            arrived(e_in.at[f, rows_of(i), :], s_p3.at[f, i], r_p3.at[f, i])

    straight = chunks - CROSS

    def hidden_step(step, carry):
        c = jnp.where(step < 2 * CROSS, step // 2 + (step % 2) * straight, step - CROSS)
        to = jnp.where(c < straight, pair, over)
        rows = rows_at(c, PIECE)
        for h in range(heads):
            kc = head_keys(h)
            vc = head_vals(h)
            full = mixed[rows, vc].astype(F32)
            full += dot(reach[rows, kc], e_in[h // group, :, head_keys(h % group)], ((1,), (1,)))
            mean = jnp.mean(full * full, axis=-1, keepdims=True)
            val = gate[rows, vc].astype(F32)
            silu = val / (1.0 + jnp.exp(-val))
            hid[rows, vc] = (full * lax.rsqrt(mean + 1e-5) * silu).astype(BF16)
        rdma(hid.at[rows, :], hid_peer.at[rows, :], s_hid.at[c], r_hid.at[c], ctx, to).start()
        return carry

    lax.fori_loop(0, 2 * CROSS, hidden_step, 0)
    stage_c(0)
    lax.fori_loop(2 * CROSS, chunks, hidden_step, 0)

    stage_c(1)
    stage_a(2)
    for load in loads[5:]:
        load.wait()
    stage_d(0)
    stage_d(1)

    tile = 512

    def columns(do):
        def column(n, carry):
            do(pl.ds(pl.multiple_of(n * tile, tile), tile))
            return carry

        lax.fori_loop(0, width // tile, column, 0, unroll=2)

    def own_sums(first, count, j):
        rows = pl.ds(first * PIECE, count * PIECE)

        def both_parts(cols):
            total = dot(hid[rows, :], wo[0, :, cols], ((1,), (0,)))
            own[rows, cols] = total + dot(hid_peer[rows, :], wp[j, :, cols], ((1,), (0,)))

        columns(both_parts)

    def piece_at(step):
        late = step - (chunks - 2 * CROSS + 1)
        crossed = jnp.logical_and(late >= 0, late % 2 == 0)
        behind_cross = step - (late + 1) // 2
        return jnp.where(late < 0, step, jnp.where(crossed, straight + late // 2, behind_cross))

    def main_step(step, carry):
        c = piece_at(step)
        crossed = c >= straight
        to = jnp.where(crossed, pair, over)
        jo = jnp.where(crossed, 2, 1)
        jp = jnp.where(crossed, 3, 1)
        rows = rows_at(c, PIECE)

        def own_part(cols):
            ahead_of[:, cols] = dot(hid[rows, :], wo[jo, :, cols], ((1,), (0,)))

        def pair_part(cols):
            total = ahead_of[:, cols] + dot(hid_peer[rows, :], wp[jp, :, cols], ((1,), (0,)))
            send[rows, cols] = total.astype(BF16)

        columns(own_part)
        arrived(hid_peer.at[rows, :], s_hid.at[c], r_hid.at[c])
        columns(pair_part)
        rdma(send.at[rows, :], recv.at[rows, :], s_rs.at[c], r_rs.at[c], ctx, to).start()

        def at(when, *actions):
            @pl.when(step == when)
            def _():
                for action, *args in actions:
                    action(*args)

        at(3, (stage_b, 2), (stage_a, 3))
        at(5, (stage_c, 2))
        at(6, (stage_b, 3), (stage_a, 4))
        at(7, (stage_d, 2), (own_sums, 0, 4, 0))
        at(8, (stage_c, 3))
        at(9, (own_sums, 4, 4, 0))
        at(10, (stage_d, 3))
        at(11, (stage_b, 4), (own_sums, 8, 4, 0))
        at(14, (stage_c, 4))
        return carry

    lax.fori_loop(0, chunks, main_step, 0)
    stage_d(4)
    own_sums(12, straight - 12, 0)
    own_sums(straight, CROSS, 2)

    for f in range(halves):
        for step in range(1, 2 * NX):
            i = (me + step) % (2 * NX)
            if f == 0:
                left(decay, s_a1.at[i], r_a1.at[i])
            left(p1.at[f, i], s_p1.at[f, i], r_p1.at[f, i])
            left(p3.at[f, i], s_p3.at[f, i], r_p3.at[f, i])
        for far in range(1, REACH + 1):

            @pl.when(z + far < NZ)
            def _():
                n = far - 1
                if f == 0:
                    left(a_out, s_a2.at[n], r_a2.at[n])
                left(t_out.at[f], s_p2.at[f, n], r_p2.at[f, n])

    for u in range(len(units)):
        weights_left(u)

    def hidden_left(c, carry):
        rows = rows_at(c, PIECE)
        left(hid.at[rows, :], s_hid.at[c], r_hid.at[c])
        return carry

    lax.fori_loop(0, chunks, hidden_left, 0)

    def result_step(step, carry):
        c = piece_at(step)
        rows = rows_at(c, PIECE)
        arrived(recv.at[rows, :], s_rs.at[c], r_rs.at[c])
        out[rows, :] = (own[rows, :] + recv[rows, :].astype(F32)).astype(BF16)

        @pl.when(step >= 2)
        def _():
            before = piece_at(step - 2)
            left(send.at[rows_at(before, PIECE), :], s_rs.at[before], r_rs.at[before])

        return carry

    lax.fori_loop(0, chunks, result_step, 0)
    for step in range(chunks - 2, chunks):
        left(send.at[rows_at(piece_at(step), PIECE), :], s_rs.at[piece_at(step)], r_rs.at[piece_at(step)])


def copy_kernel(src, dst, sems):
    parts = sems.shape[0]
    size = src.shape[0] // parts
    writes = [
        pltpu.make_async_copy(src.at[pl.ds(i * size, size)], dst.at[pl.ds(i * size, size)], sems.at[i])
        for i in range(parts)
    ]
    for write in writes:
        write.start()
    for write in writes:
        write.wait()


def shards(queries, keys, values, log_gate, out_gate, segment_ids, final_projector):
    tokens = queries.shape[0]
    keys_wide = queries.shape[1]
    vals_wide = values.shape[1]
    depth, full = final_projector.shape
    width = full // 4
    slots = 2 * NX
    part = DV // slots
    blocks = tokens // CH
    chunks = tokens // PIECE
    halves = 2
    wide = keys_wide // halves

    vm = pltpu.VMEM
    dma = pltpu.SemaphoreType.DMA
    projected = pl.pallas_call(
        layer_kernel,
        in_specs=[pl.BlockSpec(memory_space=pltpu.SMEM)] + [pl.BlockSpec(memory_space=pl.ANY)] * 6,
        out_specs=pl.BlockSpec(memory_space=pltpu.VMEM),
        out_shape=pltpu.VMEM((tokens, width), BF16),
        scratch_shapes=[
            vm((tokens, keys_wide), BF16),
            vm((tokens, keys_wide), BF16),
            vm((tokens, vals_wide), BF16),
            vm((tokens, keys_wide), BF16),
            vm((tokens, keys_wide), F32),
            vm((halves, DV, wide), F32),
            vm((halves, DV, wide), BF16),
            vm((blocks, DV, keys_wide), BF16),
            vm((blocks, 1, keys_wide), F32),
            vm((1, keys_wide), F32),
            vm((halves, 1, wide), F32),
            vm((tokens, vals_wide), BF16),
            vm((tokens, keys_wide), BF16),
            vm((tokens, vals_wide), BF16),
            vm((3, depth, width), BF16),
            vm((4, depth, width), BF16),
            vm((tokens, vals_wide), BF16),
            vm((tokens, vals_wide), BF16),
            vm((tokens, width), BF16),
            vm((tokens, width), BF16),
            vm((tokens, width), F32),
            vm((PIECE, width), F32),
            vm((halves, slots, part, wide), BF16),
            vm((slots, 1, keys_wide), F32),
            vm((halves, slots, part, wide), F32),
            vm((slots, 1, keys_wide), F32),
            vm((halves, part, wide), BF16),
            vm((1, keys_wide), F32),
            vm((halves, REACH, part, wide), BF16),
            vm((REACH, 1, keys_wide), F32),
            vm((part, wide), F32),
            vm((halves, slots, part, wide), BF16),
            vm((halves, DV, wide), BF16),
            dma((halves, slots)), dma((halves, slots)),
            dma((slots,)), dma((slots,)),
            dma((halves, REACH)), dma((halves, REACH)),
            dma((REACH,)), dma((REACH,)),
            dma((halves, slots)), dma((halves, slots)),
            dma((5,)), dma((5,)),
            dma((5, 2)), dma((5, 2)),
            dma((5, 2)), dma((5, 2)),
            dma((5, 5)), dma((5, 5)),
            dma((chunks,)), dma((chunks,)),
            dma((chunks,)), dma((chunks,)),
            dma((8,)),
        ],
        compiler_params=pltpu.CompilerParams(
            collective_id=0, has_side_effects=True, vmem_limit_bytes=58 * 2**20
        ),
    )(segment_ids, log_gate, keys, values, queries, out_gate, final_projector)
    return pl.pallas_call(
        copy_kernel,
        in_specs=[pl.BlockSpec(memory_space=pltpu.VMEM)],
        out_specs=pl.BlockSpec(memory_space=pl.ANY),
        out_shape=jax.ShapeDtypeStruct((tokens, width), BF16),
        scratch_shapes=[dma((4,))],
        compiler_params=pltpu.CompilerParams(vmem_limit_bytes=16 * 2**20),
    )(projected)


def solution(mesh):
    return jax.shard_map(
        shards,
        mesh=mesh,
        in_specs=(
            P("ctx", "head"),
            P("ctx", "head"),
            P("ctx", "head"),
            P("ctx", "head"),
            P("ctx", "head"),
            P(),
            P("head", None),
        ),
        out_specs=P("ctx", "head"),
        check_vma=False,
    )
```
